32 devices in a mesh: grp: 2 (over y), tm: 16 (over z, x, core).
Axes of the slice: x: 2, y: 2, z: 4, core: 2. Of those that a mesh axis runs over, the one named last changes fastest.
Arguments:
- residual: bfloat16 [4, 2, 4096, 2048], P('grp', None, 'tm'), parts along dimension 0, may hold values from -6 to 6
- eigenbasis: bfloat16 [2048, 2048], P('tm'), may hold values from -0.125 to 0.125
- eigenvalues: float32 [2048], replicated, may hold values from 0.05 to 5
- node_order: int32 [2048], replicated, may hold values from 0 to 2047, each once
Outputs:
- correction: float32 [4, 2, 4096, 2048], P('grp', None, 'tm'), parts along dimension 0
The draws below stay inside these ranges and needn't reach their ends.
There are 2 independent parts, one for each index of `grp`. The reference program is written for one: setup_inputs(seed, part) draws one part's arguments, and reference() takes and returns one part's arrays. A program takes and returns all parts, laid end to end along the dimension named above; an argument that names none is the same for every part. Nothing has to cross between parts.
Inputs may be any that keep to these rules, and one draw needn't show every extreme that they name: node_order names every number of 0 to 2047 exactly once.
All inputs are finite; a program needn't handle non-finite values.
Results may differ from the reference program's by a relative error of at most 0.0055.
Values may be sent and summed in bfloat16 or wider, within the bound.
A program may use at most 64 MiB of HBM per device.

```python
import math
import jax
import jax.numpy as jnp

NT = 4096
NS = 2048
FIELDS = 2
RHS = 2


def levels(stream_key, extent, split, low, top_value):
    gain, own = 1.0, jax.random.fold_in(stream_key, 6)
    for axis_at, blocks in split:
        steps = jnp.exp(jax.random.uniform(jax.random.fold_in(own, axis_at), (blocks,), jnp.float32, low / len(split), top_value / len(split)))
        gain = gain * jnp.repeat(steps, extent[axis_at] // blocks).reshape([-1 if axis == axis_at else 1 for axis in range(len(extent))])
    return gain


def gaussian(rng, dims, scale, bound, cuts=(), kind=jnp.bfloat16):
    level = levels(rng, dims, cuts, -0.22, 0.18) if cuts else 1.0
    array = jax.random.normal(rng, dims, jnp.float32) * scale * level
    return jnp.minimum(jnp.maximum(array, -bound), bound).astype(kind)


def setup_inputs(seed: int = 0, part: int = 0) -> dict:
    key_of = jax.random.split(jax.random.key(seed), 5)
    own_keys = jax.random.split(jax.random.fold_in(key_of[4], part), 5)
    residual = gaussian(own_keys[0], (RHS, FIELDS, NT, NS), 1.0, 6.0, ((2, 16),))
    eigenbasis = gaussian(key_of[1], (NS, NS), NS ** -0.5, 0.125, ((0, 16),))
    eigenvalues = jnp.clip(jnp.exp(jax.random.uniform(key_of[2], (NS,), jnp.float32, math.log(0.05), math.log(5.0))), 0.05, 5.0)
    node_order = jax.random.permutation(key_of[3], NS).astype(jnp.int32)
    return dict(residual=residual, eigenbasis=eigenbasis, eigenvalues=eigenvalues, node_order=node_order)


def sine_block(length, first_col, block_width):
    row_index = jnp.arange(length, dtype=jnp.int32)[:, None] + 1
    col_index = first_col + jnp.arange(block_width, dtype=jnp.int32)[None, :] + 1
    phase_mod = row_index * col_index % (2 * (length + 1))
    angle_rad = phase_mod.astype(jnp.float32) * (jnp.pi / (length + 1))
    return (jnp.sqrt(2.0 / (length + 1)) * jnp.sin(angle_rad)).astype(jnp.bfloat16)

def reference(residual, eigenbasis, eigenvalues, node_order):
    ordered = jnp.take(residual, node_order, axis=3)
    modal_data = jnp.einsum('sj,rfts->rfjt', eigenbasis.astype(jnp.float32), ordered.astype(jnp.float32)).astype(jnp.bfloat16)
    sine_table = sine_block(NT, 0, NT)
    flat_modal = modal_data.reshape(-1, NT)
    spectral = jnp.dot(flat_modal, sine_table, preferred_element_type=jnp.float32).reshape(RHS, FIELDS, NS, NT)
    freq_index = (jnp.arange(NT, dtype=jnp.int32) + 1).astype(jnp.float32)
    time_eigen = 4.0 * jnp.sin(freq_index * (jnp.pi / (2 * (NT + 1)))) ** 2
    shift_sum = eigenvalues[:, None] + time_eigen[None, :]
    determinant = shift_sum * shift_sum + 1.0
    state_part = (shift_sum * spectral[:, 0] - spectral[:, 1]) / determinant
    adjoint = (spectral[:, 0] + shift_sum * spectral[:, 1]) / determinant
    scaled = jnp.stack((state_part, adjoint), axis=1).astype(jnp.bfloat16)
    back_modes = jnp.dot(scaled.reshape(-1, NT), sine_table.T, preferred_element_type=jnp.float32)
    back_modes = back_modes.astype(jnp.bfloat16).reshape(RHS, FIELDS, NS, NT)
    shaped = jnp.einsum('sj,rfjt->rfts', eigenbasis.astype(jnp.float32), back_modes.astype(jnp.float32))
    correction = jnp.zeros(shaped.shape, jnp.float32).at[:, :, :, node_order].set(shaped)
    return correction
```

```python
import functools

import jax
import jax.numpy as jnp
from jax import lax
from jax.experimental import pallas as pl
from jax.experimental.pallas import tpu as pltpu
from jax.sharding import PartitionSpec as P

SEGMENTS = 8
BLOCKS = 4
MESH = pl.DeviceIdType.MESH
F32, BF16 = jnp.float32, jnp.bfloat16


def mul(a, b):
    return a[0] * b[0] - a[1] * b[1], a[0] * b[1] + a[1] * b[0]


def add(a, b):
    return a[0] + b[0], a[1] + b[1]


def sub(a, b):
    return a[0] - b[0], a[1] - b[1]


def inverse_of(a):
    size = a[0] * a[0] + a[1] * a[1]
    return a[0] / size, -a[1] / size


def power(a, exponent):
    result, square = None, a
    while exponent:
        if exponent & 1:
            result = square if result is None else mul(result, square)
        exponent >>= 1
        if exponent:
            square = mul(square, square)
    return result


def decay_root(mu):
    wide = 2.0 + mu
    disc_re, disc_im = wide * wide - 5.0, -2.0 * wide
    size = jnp.sqrt(disc_re * disc_re + disc_im * disc_im)
    sqrt_re = jnp.sqrt(0.5 * (size + disc_re))
    sqrt_im = 0.5 * disc_im / sqrt_re
    half = inverse_of((wide + sqrt_re, sqrt_im - 1.0))
    return 2.0 * half[0], 2.0 * half[1]


def time_order(steps, transposed):
    per_seg = steps // SEGMENTS
    row = lax.broadcasted_iota(jnp.int32, (steps, steps), 1 if transposed else 0)
    col = lax.broadcasted_iota(jnp.int32, (steps, steps), 0 if transposed else 1)
    time = (row % SEGMENTS) * per_seg + row // SEGMENTS
    return jnp.where(time == col, 1.0, 0.0).astype(BF16)


def forward_kernel(
    chips, basis_ref, node_ref, mu_ref, unit_mu_ref, residual_ref,
    moved_out, z_out, seg_out, edge_out,
    held, choose, moved, rows_in, z, devs, devs_in, edges, edges_in,
    local_sem, pair_send, pair_recv, ring_send, ring_recv, y_send, y_recv,
    block_send, block_recv, dev_send, dev_recv, edge_send, edge_recv,
):
    vectors, fields, steps, states = residual_ref.shape
    rows, modes = basis_ref.shape
    width = moved.shape[3]
    piece = width // 2
    half_modes = modes // 2
    owners, lanes = devs.shape[0], devs.shape[3]
    parts = 2 * chips
    half = chips // 2
    per_seg = steps // SEGMENTS

    me, group = lax.axis_index("tm"), lax.axis_index("grp")
    core, chip = me % 2, me // 2
    other = 1 - core
    odd = chip % 2
    place = (1 - odd) * (chip // 2) + odd * (chips - 1 - chip // 2)

    def chip_at(position):
        position = (position + chips) % chips
        second = position // half
        return (1 - second) * 2 * position + second * (2 * (chips - 1 - position) + 1)

    targets = (chip_at(place + 1) * 2 + core, chip_at(place - 1) * 2 + core)
    pair = {"tm": chip * 2 + other}
    across = {"grp": 1 - group}
    order = (group, 1 - group, 2, 3)
    ring_blocks = (group, 2, 3)

    def load_rows(r, f):
        return pltpu.make_async_copy(residual_ref.at[r, f], rows_in.at[r, f], local_sem.at[8 + r * fields + f])

    def own_rows(b, i):
        columns = pl.ds(pl.multiple_of(core * half_modes + b * width + i * piece, piece), piece)
        return pltpu.make_async_copy(
            basis_ref.at[:, columns], held.at[b, i, chip, pl.ds(pl.multiple_of(core * rows, rows), rows)],
            local_sem.at[b * 2 + i],
        )

    def pair_rows(b, i, side, whose):
        columns = pl.ds(pl.multiple_of(side * half_modes + b * width + i * piece, piece), piece)
        return pltpu.make_async_remote_copy(
            src_ref=basis_ref.at[:, columns],
            dst_ref=held.at[b, i, chip, pl.ds(pl.multiple_of(whose * rows, rows), rows)],
            send_sem=pair_send.at[b * 2 + i], recv_sem=pair_recv.at[b * 2 + i],
            device_id=pair, device_id_type=MESH,
        )

    def ring(turn, s, d, i, behind):
        source = chip_at(place - (s - 1 + behind)) if d == 0 else chip_at(place + (s - 1 + behind))
        ref = held.at[ring_blocks[turn], i, source]
        at = (turn * 2 + d) * 2 + i
        return pltpu.make_async_remote_copy(
            src_ref=ref, dst_ref=ref, send_sem=ring_send.at[at, s - 1], recv_sem=ring_recv.at[at, s - 1],
            device_id={"tm": targets[d]}, device_id_type=MESH,
        )

    def over_y(i, source, b):
        ref = held.at[b, i, source]
        return pltpu.make_async_remote_copy(
            src_ref=ref, dst_ref=ref, send_sem=y_send.at[i, source], recv_sem=y_recv.at[i, source],
            device_id=across, device_id_type=MESH,
        )

    BOTH = ((0, 0), (0, 1), (1, 0), (1, 1))
    LAST = ((0, 0), (1, 1))

    def first_sends(turn):
        for d, i in (BOTH if half > 1 else LAST):
            ring(turn, 1, d, i, 0).start()

    def event(turn, s, kind):
        for d, i in (LAST if kind == "last" else BOTH):
            ring(turn, s, d, i, 1).wait_recv()
            if kind == "mid" or (kind == "next_last" and i == d):
                ring(turn, s + 1, d, i, 0).start()
            if turn == 0:
                source = chip_at(place - s) if d == 0 else chip_at(place + s)
                over_y(i, source, group).start()

    def phase(turn, p):
        if p == 0:
            if half - 3 == 1:
                event(turn, 1, "mid")
            elif half > 4:
                def body(s, carry):
                    event(turn, s, "mid")
                    return carry
                lax.fori_loop(1, half - 2, body, 0)
        elif half - 3 + p >= 1:
            event(turn, half - 3 + p, ("", "mid", "next_last", "last")[p])

    def build_choose(lo, hi):
        tile = min(256, states)

        def one(t, carry):
            start = pl.multiple_of(t * tile, tile)
            index = lax.broadcasted_iota(jnp.int32, (tile, states), 0) + start
            choose[pl.ds(start, tile), :] = jnp.where(index == node_ref[...], 1.0, 0.0).astype(BF16)
            return carry

        count = states // tile
        lax.fori_loop(lo * count // 4, hi * count // 4, one, 0)

    def order_rows(r):
        tile = min(512, states)
        perm = time_order(steps, False)
        for f in range(fields):
            load_rows(r, f).wait()

        def one(t, carry):
            here = pl.ds(pl.multiple_of(t * tile, tile), tile)
            for f in range(fields):
                rows_in[r, f, :, here] = jnp.dot(
                    perm, rows_in[r, f, :, here], preferred_element_type=F32
                ).astype(BF16)
            return carry

        lax.fori_loop(0, states // tile, one, 0)

    def permute(b):
        tile = min(512, states)

        def one(t, carry):
            here = pl.ds(pl.multiple_of(t * tile, tile), tile)
            moved[core, b, here, :] = jnp.dot(
                choose[here, :], jnp.concatenate([held[b, i].reshape(states, piece) for i in range(2)], axis=1),
                preferred_element_type=F32,
            ).astype(BF16)
            return carry

        lax.fori_loop(0, states // tile, one, 0)

    def hand_over(b, side):
        ref = moved.at[side, b]
        return pltpu.make_async_remote_copy(
            src_ref=ref, dst_ref=ref, send_sem=block_send.at[b], recv_sem=block_recv.at[b],
            device_id=pair, device_id_type=MESH,
        )

    def store_moved(h, b):
        return pltpu.make_async_copy(moved.at[h, b], moved_out.at[h, b], local_sem.at[8 + vectors * fields + h * BLOCKS + b])

    def store_z(h, b):
        return pltpu.make_async_copy(z.at[h, b], z_out.at[h, b], local_sem.at[8 + vectors * fields + (2 + h) * BLOCKS + b])

    def to_modes(h, b):
        root = decay_root(mu_ref[h, b])
        root8 = tuple(jnp.broadcast_to(x, (SEGMENTS, width)) for x in root)
        jump = power(root, per_seg)

        def one(r, carry):
            for f in range(fields):
                z[h, b, r, f] = jnp.dot(rows_in[r, f], moved[h, b], preferred_element_type=F32).astype(BF16)

            def pairs(k):
                both = pl.ds(k * SEGMENTS, 2 * SEGMENTS)
                full = [z[h, b, r, f, both, :].astype(F32) for f in range(2)]
                return [tuple(x[m * SEGMENTS:(m + 1) * SEGMENTS] for x in full) for m in range(2)]

            low, high = pairs(0), pairs(per_seg - 2)
            ahead = add(low[1], mul(root8, low[0]))
            behind = add(high[0], mul(root8, high[1]))
            for k in range(2, per_seg, 2):
                low, high = pairs(k), pairs(per_seg - 2 - k)
                ahead = add(low[0], mul(root8, ahead))
                ahead = add(low[1], mul(root8, ahead))
                behind = add(high[1], mul(root8, behind))
                behind = add(high[0], mul(root8, behind))
            for c in range(2):
                seg_out[h, b, r, 0, c] = ahead[c]
                seg_out[h, b, r, 1, c] = behind[c]
            row = lambda a, s: (a[0][s:s + 1], a[1][s:s + 1])
            front, back = row(ahead, 0), row(behind, SEGMENTS - 1)
            for s in range(1, SEGMENTS):
                front = add(row(ahead, s), mul(jump, front))
                back = add(row(behind, SEGMENTS - 1 - s), mul(jump, back))
            slab = (h * half_modes + b * width) // lanes
            for j in range(width // lanes):
                cut = slice(j * lanes, (j + 1) * lanes)
                for c in range(2):
                    devs[slab + j, r, c:c + 1, :] = front[c][:, cut]
                    devs[slab + j, r, 2 + c:3 + c, :] = back[c][:, cut]
            return carry

        lax.fori_loop(0, vectors, one, 0)
        store_z(h, b).start()

    def send_devs(e):
        return pltpu.make_async_remote_copy(
            src_ref=devs.at[e], dst_ref=devs_in.at[me], send_sem=dev_send.at[e], recv_sem=dev_recv.at[me],
            device_id={"tm": e}, device_id_type=MESH,
        )

    def devs_from(d):
        return pltpu.make_async_remote_copy(
            src_ref=devs.at[0], dst_ref=devs_in.at[d], send_sem=dev_send.at[0], recv_sem=dev_recv.at[d],
            device_id=pair, device_id_type=MESH,
        )

    def send_edges(d):
        return pltpu.make_async_remote_copy(
            src_ref=edges.at[d], dst_ref=edges_in.at[me], send_sem=edge_send.at[d], recv_sem=edge_recv.at[me],
            device_id={"tm": d}, device_id_type=MESH,
        )

    def edges_from(e):
        return pltpu.make_async_remote_copy(
            src_ref=edges.at[0], dst_ref=edges_in.at[e], send_sem=edge_send.at[0], recv_sem=edge_recv.at[e],
            device_id=pair, device_id_type=MESH,
        )

    def others(count, act):
        def body(k, carry):
            d = (me + k) % parts
            if count == parts:
                act(d)
            else:
                pl.when(d < count)(lambda: act(d))
            return carry

        lax.fori_loop(1, parts, body, 0)

    def if_owner(act):
        if owners == parts:
            act()
        else:
            pl.when(me < owners)(act)

    def couple():
        root = decay_root(unit_mu_ref[me])
        hop = power(root, steps)
        whole = mul(power(hop, parts), root)
        square = mul(whole, whole)
        scale = mul(root, inverse_of((1.0 - square[0], -square[1])))
        zero = jnp.zeros((1, lanes), F32)
        for r in range(vectors):
            row = lambda ref, d, c: (ref[d, r, c:c + 1, :], ref[d, r, c + 1:c + 2, :])

            def scan(k, carry):
                left, right = carry
                d = parts - 1 - k
                for c in range(2):
                    edges[k, r, c:c + 1, :] = left[c]
                    edges[d, r, 2 + c:3 + c, :] = right[c]
                return add(row(devs_in, k, 0), mul(hop, left)), add(row(devs_in, d, 2), mul(hop, right))

            all_left, all_right = lax.fori_loop(0, parts, scan, ((zero, zero), (zero, zero)))
            start_term = mul(scale, sub(all_right, mul(whole, all_left)))
            end_term = mul(scale, sub(all_left, mul(whole, all_right)))

            def correct(k, carry):
                start_term, end_term = carry
                d = parts - 1 - k
                left, right = sub(row(edges, k, 0), start_term), sub(row(edges, d, 2), end_term)
                for c in range(2):
                    edges[k, r, c:c + 1, :] = left[c]
                    edges[d, r, 2 + c:3 + c, :] = right[c]
                return mul(hop, start_term), mul(hop, end_term)

            lax.fori_loop(0, parts, correct, (start_term, end_term))

    for r in range(vectors):
        for f in range(fields):
            load_rows(r, f).start()
    for b in range(BLOCKS):
        for i in range(2):
            own_rows(b, i).start()

    barrier = pltpu.get_barrier_semaphore()

    def greet(k, carry):
        pl.semaphore_signal(barrier, inc=1, device_id={"tm": (me + k) % parts}, device_id_type=MESH)
        return carry

    lax.fori_loop(1, parts, greet, 0)
    pl.semaphore_signal(barrier, inc=1, device_id=across, device_id_type=MESH)
    pl.semaphore_wait(barrier, parts)

    for b in order:
        for i in range(2):
            pair_rows(b, i, other, core).start()
    for b in ring_blocks[:1]:
        for i in range(2):
            own_rows(b, i).wait()
            pair_rows(b, i, core, other).wait_recv()
    first_sends(0)
    build_choose(0, 2)
    for b in order[1:]:
        for i in range(2):
            own_rows(b, i).wait()
            pair_rows(b, i, core, other).wait_recv()
    phase(0, 0)
    first_sends(1)
    build_choose(2, 4)
    phase(0, 1)
    order_rows(0)
    phase(1, 0)
    for r in range(1, vectors):
        order_rows(r)
    phase(0, 2)
    first_sends(2)
    phase(1, 1)
    phase(0, 3)

    def own_half(b):
        hand_over(b, core).start()
        store_moved(core, b).start()
        to_modes(core, b)

    def pair_half(b):
        hand_over(b, other).wait_recv()
        store_moved(other, b).start()
        to_modes(other, b)

    permute(group)
    phase(1, 2)
    own_half(group)
    phase(2, 0)
    pair_half(group)
    phase(1, 3)

    def from_y(k, carry):
        source = chip_at(place + k)
        for i in range(2):
            over_y(i, source, 1 - group).wait_recv()
        return carry

    lax.fori_loop(1, chips, from_y, 0)
    permute(1 - group)
    phase(2, 1)
    own_half(1 - group)
    phase(2, 2)
    pair_half(1 - group)
    permute(2)
    phase(2, 3)
    permute(3)
    own_half(2)
    pair_half(2)
    own_half(3)
    pair_half(3)

    others(owners, lambda e: send_devs(e).start())

    def settle():
        devs_in[me] = devs[me]
        others(parts, lambda d: devs_from(d).wait_recv())
        couple()
        others(parts, lambda d: send_edges(d).start())
        edges_in[me] = edges[me]

    if_owner(settle)
    others(owners, lambda e: edges_from(e).wait_recv())
    edge_out[...] = edges_in[...]

    others(owners, lambda e: send_devs(e).wait_send())
    if_owner(lambda: others(parts, lambda d: send_edges(d).wait_send()))
    for b in order:
        for i in range(2):
            pair_rows(b, i, other, core).wait_send()
        hand_over(b, core).wait_send()
        for h in range(2):
            store_moved(h, b).wait()
            store_z(h, b).wait()
    for turn in range(3):
        def drain(s, carry):
            for d, i in BOTH:
                ring(turn, s, d, i, 0).wait_send()
            return carry

        lax.fori_loop(1, half, drain, 0)
        for d, i in LAST:
            ring(turn, half, d, i, 0).wait_send()

    def y_drain(k, carry):
        source = chip_at(place + k)
        for i in range(2):
            over_y(i, source, group).wait_send()
        return carry

    lax.fori_loop(1, chips, y_drain, 0)


def backward_kernel(z_ref, seg_ref, edge_ref, mu_ref, moved_ref, out_ref, p_ref, u_ref, back_ref):
    _, _, vectors, fields, steps, width = z_ref.shape
    states = out_ref.shape[3]
    per_seg = steps // SEGMENTS
    slabs, lanes = edge_ref.shape[2], edge_ref.shape[5]
    perm = time_order(steps, True)
    for h in range(2):
        root = decay_root(mu_ref[h, 0])
        root8 = tuple(jnp.broadcast_to(x, (SEGMENTS, width)) for x in root)
        jump = power(root, per_seg)
        square = mul(root, root)
        gain = mul(root, inverse_of((1.0 - square[0], -square[1])))

        def edge(r, c):
            return jnp.concatenate([edge_ref[h, 0, j, r, c:c + 1, :] for j in range(slabs)], axis=1)

        for r in range(vectors):
            row = lambda a, s: (seg_ref[h, 0, r, a, 0, s:s + 1, :], seg_ref[h, 0, r, a, 1, s:s + 1, :])
            lefts = [(edge(r, 0), edge(r, 1))]
            rights = [(edge(r, 2), edge(r, 3))]
            for s in range(SEGMENTS):
                lefts.append(add(row(0, s), mul(jump, lefts[-1])))
            for s in range(SEGMENTS - 1, 0, -1):
                rights.append(add(row(1, s), mul(jump, rights[-1])))
            rights = rights[::-1]
            ends = [mul(gain, add(rights[s], mul(root, lefts[s + 1]))) for s in range(SEGMENTS)]
            stack = lambda rows: tuple(jnp.concatenate([x[c] for x in rows], axis=0) for c in range(2))
            p = stack(lefts[:SEGMENTS])
            for k in range(0, per_seg, 2):
                both = pl.ds(k * SEGMENTS, 2 * SEGMENTS)
                pair = [z_ref[h, 0, r, f, both, :].astype(F32) for f in range(2)]
                for m in range(2):
                    here = tuple(x[m * SEGMENTS:(m + 1) * SEGMENTS] for x in pair)
                    p = add(here, mul(root8, p))
                    for c in range(2):
                        p_ref[c, pl.ds((k + m) * SEGMENTS, SEGMENTS), :] = p[c]
            u = stack(ends)
            for k in range(per_seg - 2, -1, -2):
                later = []
                for m in (1, 0):
                    here = pl.ds((k + m) * SEGMENTS, SEGMENTS)
                    u = mul(root8, add((p_ref[0, here, :], p_ref[1, here, :]), u))
                    later.append(u)
                both = pl.ds(k * SEGMENTS, 2 * SEGMENTS)
                for c in range(2):
                    u_ref[c, both, :] = jnp.concatenate([later[1][c], later[0][c]], axis=0).astype(BF16)
            for c in range(2):
                back_ref[r, c, :, h * width:(h + 1) * width] = jnp.dot(
                    perm, u_ref[c], preferred_element_type=F32
                ).astype(BF16)

    tile = min(256, states)
    step = pl.program_id(0)

    def accumulate(first):
        def one(t, carry):
            here = pl.ds(pl.multiple_of(t * tile, tile), tile)
            block = jnp.concatenate([moved_ref[h, 0, here, :] for h in range(2)], axis=1)
            for r in range(vectors):
                for f in range(fields):
                    part = lax.dot_general(
                        back_ref[r, f], block, (((1,), (1,)), ((), ())), preferred_element_type=F32
                    )
                    out_ref[r, f, :, here] = part if first else out_ref[r, f, :, here] + part
            return carry

        lax.fori_loop(0, states // tile, one, 0)

    pl.when(step == 0)(lambda: accumulate(True))
    pl.when(step > 0)(lambda: accumulate(False))


def on_device(residual, eigenbasis, eigenvalues, node_order):
    vectors, fields, steps, states = residual.shape
    rows, modes = eigenbasis.shape
    parts = lax.axis_size("tm")
    chips = parts // 2
    width = modes // (2 * BLOCKS)
    owners = min(parts, modes // 128)
    lanes = modes // owners
    slabs = width // lanes
    vm, anyspace = pl.BlockSpec(memory_space=pltpu.VMEM), pl.BlockSpec(memory_space=pl.ANY)
    dma = pltpu.SemaphoreType.DMA
    mu = eigenvalues.reshape(2, BLOCKS, 1, width)
    moved, z, seg, edge = pl.pallas_call(
        functools.partial(forward_kernel, chips),
        out_shape=[
            jax.ShapeDtypeStruct((2, BLOCKS, states, width), BF16),
            jax.ShapeDtypeStruct((2, BLOCKS, vectors, fields, steps, width), BF16),
            jax.ShapeDtypeStruct((2, BLOCKS, vectors, 2, 2, SEGMENTS, width), F32),
            jax.ShapeDtypeStruct((owners, vectors, 4, lanes), F32),
        ],
        in_specs=[anyspace, vm, vm, vm, anyspace],
        out_specs=[anyspace, anyspace, vm, vm],
        scratch_shapes=[
            pltpu.VMEM((BLOCKS, 2, chips, 2 * rows, width // 2), BF16),
            pltpu.VMEM((states, states), BF16),
            pltpu.VMEM((2, BLOCKS, states, width), BF16),
            pltpu.VMEM((vectors, fields, steps, states), BF16),
            pltpu.VMEM((2, BLOCKS, vectors, fields, steps, width), BF16),
            pltpu.VMEM((owners, vectors, 4, lanes), F32),
            pltpu.VMEM((parts, vectors, 4, lanes), F32),
            pltpu.VMEM((parts, vectors, 4, lanes), F32),
            pltpu.VMEM((owners, vectors, 4, lanes), F32),
            dma((8 + vectors * fields + 4 * BLOCKS,)),
            dma((8,)), dma((8,)),
            dma((12, chips // 2)), dma((12, chips // 2)),
            dma((2, chips)), dma((2, chips)),
            dma((BLOCKS,)), dma((BLOCKS,)),
            dma((owners,)), dma((parts,)), dma((parts,)), dma((owners,)),
        ],
        compiler_params=pltpu.CompilerParams(
            collective_id=0, has_side_effects=True, vmem_limit_bytes=50 * 1024 * 1024
        ),
        name="forward",
    )(eigenbasis, node_order.reshape(1, states), mu, eigenvalues.reshape(owners, 1, lanes), residual)

    return pl.pallas_call(
        backward_kernel,
        grid=(BLOCKS,),
        in_specs=[
            pl.BlockSpec((2, 1, vectors, fields, steps, width), lambda b: (0, b, 0, 0, 0, 0)),
            pl.BlockSpec((2, 1, vectors, 2, 2, SEGMENTS, width), lambda b: (0, b, 0, 0, 0, 0, 0)),
            pl.BlockSpec((2, 1, slabs, vectors, 4, lanes), lambda b: (0, b, 0, 0, 0, 0)),
            pl.BlockSpec((2, 1, 1, width), lambda b: (0, b, 0, 0)),
            pl.BlockSpec((2, 1, states, width), lambda b: (0, b, 0, 0)),
        ],
        out_specs=pl.BlockSpec((vectors, fields, steps, states), lambda b: (0, 0, 0, 0)),
        out_shape=jax.ShapeDtypeStruct((vectors, fields, steps, states), F32),
        scratch_shapes=[
            pltpu.VMEM((2, steps, width), F32),
            pltpu.VMEM((2, steps, width), BF16),
            pltpu.VMEM((vectors, fields, steps, 2 * width), BF16),
        ],
        compiler_params=pltpu.CompilerParams(vmem_limit_bytes=50 * 1024 * 1024),
        name="backward",
    )(z, seg, edge.reshape(2, BLOCKS, slabs, vectors, 4, lanes), mu, moved)


def solution(mesh):
    placed = (P("grp", None, "tm", None), P("tm", None), P(), P())
    return jax.shard_map(
        on_device, mesh=mesh, in_specs=placed, out_specs=P("grp", None, "tm", None), check_vma=False
    )
```

```python
import functools

import jax
import jax.numpy as jnp
from jax import lax
from jax.experimental import pallas as pl
from jax.experimental.pallas import tpu as pltpu
from jax.sharding import PartitionSpec as P

SEGMENTS = 8
BLOCKS = 4
VMEM_BYTES = 62 * 1024 * 1024
MESH = pl.DeviceIdType.MESH
F32, BF16 = jnp.float32, jnp.bfloat16


def mul(a, b):
    return a[0] * b[0] - a[1] * b[1], a[0] * b[1] + a[1] * b[0]


def add(a, b):
    return a[0] + b[0], a[1] + b[1]


def sub(a, b):
    return a[0] - b[0], a[1] - b[1]


def inverse_of(a):
    size = a[0] * a[0] + a[1] * a[1]
    return a[0] / size, -a[1] / size


def power(a, exponent):
    result, square = None, a
    while exponent:
        if exponent & 1:
            result = square if result is None else mul(result, square)
        exponent >>= 1
        if exponent:
            square = mul(square, square)
    return result


def decay_root(mu):
    wide = 2.0 + mu
    disc_re, disc_im = wide * wide - 5.0, -2.0 * wide
    size = jnp.sqrt(disc_re * disc_re + disc_im * disc_im)
    sqrt_re = jnp.sqrt(0.5 * (size + disc_re))
    sqrt_im = 0.5 * disc_im / sqrt_re
    half = inverse_of((wide + sqrt_re, sqrt_im - 1.0))
    return 2.0 * half[0], 2.0 * half[1]


def time_order(steps, transposed):
    per_seg = steps // SEGMENTS
    row = lax.broadcasted_iota(jnp.int32, (steps, steps), 1 if transposed else 0)
    col = lax.broadcasted_iota(jnp.int32, (steps, steps), 0 if transposed else 1)
    time = (row % SEGMENTS) * per_seg + row // SEGMENTS
    return jnp.where(time == col, 1.0, 0.0).astype(BF16)


def forward_kernel(
    chips, basis_ref, node_ref, mu_ref, unit_mu_ref, residual_ref,
    moved_out, z_out, seg_out, edge_out,
    held, choose, moved, rows_in, z, devs, devs_in, edges, edges_in,
    local_sem, pair_send, pair_recv, ring_send, ring_recv, y_send, y_recv,
    block_send, block_recv, dev_send, dev_recv, edge_send, edge_recv,
):
    vectors, fields, steps, states = residual_ref.shape
    rows, modes = basis_ref.shape
    width = moved.shape[3]
    piece = width // 2
    half_modes = modes // 2
    owners, lanes = devs.shape[0], devs.shape[3]
    parts = 2 * chips
    half = chips // 2
    per_seg = steps // SEGMENTS

    me, group = lax.axis_index("tm"), lax.axis_index("grp")
    core, chip = me % 2, me // 2
    other = 1 - core
    odd = chip % 2
    place = (1 - odd) * (chip // 2) + odd * (chips - 1 - chip // 2)

    def chip_at(position):
        position = (position + chips) % chips
        second = position // half
        return (1 - second) * 2 * position + second * (2 * (chips - 1 - position) + 1)

    targets = (chip_at(place + 1) * 2 + core, chip_at(place - 1) * 2 + core)
    pair = {"tm": chip * 2 + other}
    across = {"grp": 1 - group}
    order = (group, 1 - group, 2, 3)
    ring_blocks = (group, 2, 3)

    def part(r, f):
        return pl.ds(pl.multiple_of((r * fields + f) * steps, steps), steps)

    def load_rows(r, f):
        return pltpu.make_async_copy(residual_ref.at[r, f], rows_in.at[part(r, f)], local_sem.at[8 + r * fields + f])

    def own_rows(b, i):
        columns = pl.ds(pl.multiple_of(core * half_modes + b * width + i * piece, piece), piece)
        return pltpu.make_async_copy(
            basis_ref.at[:, columns], held.at[b, i, chip, pl.ds(pl.multiple_of(core * rows, rows), rows)],
            local_sem.at[b * 2 + i],
        )

    def pair_rows(b, i, side, whose):
        columns = pl.ds(pl.multiple_of(side * half_modes + b * width + i * piece, piece), piece)
        return pltpu.make_async_remote_copy(
            src_ref=basis_ref.at[:, columns],
            dst_ref=held.at[b, i, chip, pl.ds(pl.multiple_of(whose * rows, rows), rows)],
            send_sem=pair_send.at[b * 2 + i], recv_sem=pair_recv.at[b * 2 + i],
            device_id=pair, device_id_type=MESH,
        )

    def ring(turn, s, d, i, behind):
        source = chip_at(place - (s - 1 + behind)) if d == 0 else chip_at(place + (s - 1 + behind))
        ref = held.at[ring_blocks[turn], i, source]
        at = (turn * 2 + d) * 2 + i
        return pltpu.make_async_remote_copy(
            src_ref=ref, dst_ref=ref, send_sem=ring_send.at[at, s - 1], recv_sem=ring_recv.at[at, s - 1],
            device_id={"tm": targets[d]}, device_id_type=MESH,
        )

    def over_y(i, source, b):
        ref = held.at[b, i, source]
        return pltpu.make_async_remote_copy(
            src_ref=ref, dst_ref=ref, send_sem=y_send.at[i, source], recv_sem=y_recv.at[i, source],
            device_id=across, device_id_type=MESH,
        )

    BOTH = ((0, 0), (1, 0), (0, 1), (1, 1))
    LAST = ((0, 0), (1, 1))

    def first_sends(turn):
        for d, i in (BOTH if half > 1 else LAST):
            ring(turn, 1, d, i, 0).start()

    def event(turn, s, kind):
        for d, i in (LAST if kind == "last" else BOTH):
            ring(turn, s, d, i, 1).wait_recv()
            if kind == "mid" or (kind == "next_last" and i == d):
                ring(turn, s + 1, d, i, 0).start()
            if turn == 0:
                source = chip_at(place - s) if d == 0 else chip_at(place + s)
                over_y(i, source, group).start()

    def phase(turn, p):
        if p == 0:
            if half - 3 == 1:
                event(turn, 1, "mid")
            elif half > 4:
                def body(s, carry):
                    event(turn, s, "mid")
                    return carry
                lax.fori_loop(1, half - 2, body, 0)
        elif half - 3 + p >= 1:
            event(turn, half - 3 + p, ("", "mid", "next_last", "last")[p])

    def build_choose(lo, hi):
        tile = min(256, states)

        def one(t, carry):
            start = pl.multiple_of(t * tile, tile)
            index = lax.broadcasted_iota(jnp.int32, (tile, states), 0) + start
            choose[pl.ds(start, tile), :] = jnp.where(index == node_ref[...], 1.0, 0.0).astype(BF16)
            return carry

        count = states // tile
        lax.fori_loop(lo * count // 4, hi * count // 4, one, 0)

    def order_rows(r):
        tile = min(512, states)
        perm = time_order(steps, False)
        for f in range(fields):
            load_rows(r, f).wait()

        def one(t, carry):
            here = pl.ds(pl.multiple_of(t % (states // tile) * tile, tile), tile)
            rows_in[part(r, t // (states // tile)), here] = jnp.dot(
                perm, rows_in[part(r, t // (states // tile)), here], preferred_element_type=F32
            ).astype(BF16)
            return carry

        lax.fori_loop(0, fields * (states // tile), one, 0)

    def permute(b):
        tile = min(1024, states)

        def one(t, carry):
            here = pl.ds(pl.multiple_of(t * tile, tile), tile)
            block = jnp.concatenate([held[b, i].reshape(states, piece) for i in range(2)], axis=1)
            moved[core, b, here, :] = jnp.dot(choose[here, :], block, preferred_element_type=F32).astype(BF16)
            return carry

        lax.fori_loop(0, states // tile, one, 0)

    def hand_over(b, side):
        ref = moved.at[side, b]
        return pltpu.make_async_remote_copy(
            src_ref=ref, dst_ref=ref, send_sem=block_send.at[b], recv_sem=block_recv.at[b],
            device_id=pair, device_id_type=MESH,
        )

    def store_moved(h, b):
        return pltpu.make_async_copy(moved.at[h, b], moved_out.at[h, b], local_sem.at[8 + vectors * fields + h * BLOCKS + b])

    def store_z(h, b):
        return pltpu.make_async_copy(z.at[h, b], z_out.at[h, b], local_sem.at[8 + vectors * fields + (2 + h) * BLOCKS + b])

    def to_modes(h, b):
        root = decay_root(mu_ref[h, b])
        root8 = tuple(jnp.broadcast_to(x, (SEGMENTS, width)) for x in root)
        jump = power(root, per_seg)

        z[h, b] = jnp.dot(rows_in[...], moved[h, b], preferred_element_type=F32).astype(BF16)

        def pairs(r, k):
            at = [(r * fields + f) * steps + k * SEGMENTS for f in range(2)]
            full = [z[h, b, at[f]:at[f] + 2 * SEGMENTS, :].astype(F32) for f in range(2)]
            return [tuple(x[m * SEGMENTS:(m + 1) * SEGMENTS] for x in full) for m in range(2)]

        every = range(vectors)
        low, high = [pairs(r, 0) for r in every], [pairs(r, per_seg - 2) for r in every]
        ahead = [add(low[r][1], mul(root8, low[r][0])) for r in every]
        behind = [add(high[r][0], mul(root8, high[r][1])) for r in every]
        for k in range(2, per_seg, 2):
            low, high = [pairs(r, k) for r in every], [pairs(r, per_seg - 2 - k) for r in every]
            for m in range(2):
                ahead = [add(low[r][m], mul(root8, ahead[r])) for r in every]
                behind = [add(high[r][1 - m], mul(root8, behind[r])) for r in every]
        slab = (h * half_modes + b * width) // lanes
        row = lambda a, s: (a[0][s:s + 1], a[1][s:s + 1])
        front, back = [row(ahead[r], 0) for r in every], [row(behind[r], SEGMENTS - 1) for r in every]
        for s in range(1, SEGMENTS):
            front = [add(row(ahead[r], s), mul(jump, front[r])) for r in every]
            back = [add(row(behind[r], SEGMENTS - 1 - s), mul(jump, back[r])) for r in every]
        for r in every:
            for c in range(2):
                seg_out[h, b, r, 0, c] = ahead[r][c]
                seg_out[h, b, r, 1, c] = behind[r][c]
                for j in range(width // lanes):
                    cut = slice(j * lanes, (j + 1) * lanes)
                    devs[slab + j, c, r:r + 1, :] = front[r][c][:, cut]
                    devs[slab + j, 2 + c, r:r + 1, :] = back[r][c][:, cut]
        store_z(h, b).start()

    def send_devs(e):
        return pltpu.make_async_remote_copy(
            src_ref=devs.at[e], dst_ref=devs_in.at[me], send_sem=dev_send.at[e], recv_sem=dev_recv.at[me],
            device_id={"tm": e}, device_id_type=MESH,
        )

    def devs_from(d):
        return pltpu.make_async_remote_copy(
            src_ref=devs.at[0], dst_ref=devs_in.at[d], send_sem=dev_send.at[0], recv_sem=dev_recv.at[d],
            device_id=pair, device_id_type=MESH,
        )

    def send_edges(d):
        return pltpu.make_async_remote_copy(
            src_ref=edges.at[d], dst_ref=edges_in.at[me], send_sem=edge_send.at[d], recv_sem=edge_recv.at[me],
            device_id={"tm": d}, device_id_type=MESH,
        )

    def edges_from(e):
        return pltpu.make_async_remote_copy(
            src_ref=edges.at[0], dst_ref=edges_in.at[e], send_sem=edge_send.at[0], recv_sem=edge_recv.at[e],
            device_id=pair, device_id_type=MESH,
        )

    def others(count, act):
        def body(k, carry):
            d = (me + k) % parts
            if count == parts:
                act(d)
            else:
                pl.when(d < count)(lambda: act(d))
            return carry

        lax.fori_loop(1, parts, body, 0)

    def if_owner(act):
        if owners == parts:
            act()
        else:
            pl.when(me < owners)(act)

    def couple():
        root = decay_root(unit_mu_ref[me])
        hop = power(root, steps)
        whole = mul(power(hop, parts), root)
        square = mul(whole, whole)
        scale = mul(root, inverse_of((1.0 - square[0], -square[1])))
        zero = jnp.zeros((vectors, lanes), F32)

        def each(step, carry):
            if parts > 32:
                return lax.fori_loop(0, parts, step, carry)
            for k in range(parts):
                carry = step(k, carry)
            return carry

        def row(ref, d, c):
            return ref[d, c], ref[d, c + 1]

        def scan(k, carry):
            left, right = carry
            d = parts - 1 - k
            for c in range(2):
                edges[k, c] = left[c]
                edges[d, 2 + c] = right[c]
            return add(row(devs_in, k, 0), mul(hop, left)), add(row(devs_in, d, 2), mul(hop, right))

        all_left, all_right = each(scan, ((zero, zero), (zero, zero)))
        start_term = mul(scale, sub(all_right, mul(whole, all_left)))
        end_term = mul(scale, sub(all_left, mul(whole, all_right)))

        def correct(k, carry):
            start_term, end_term = carry
            d = parts - 1 - k
            left, right = sub(row(edges, k, 0), start_term), sub(row(edges, d, 2), end_term)
            for c in range(2):
                edges[k, c] = left[c]
                edges[d, 2 + c] = right[c]
            return mul(hop, start_term), mul(hop, end_term)

        each(correct, (start_term, end_term))

    for r in range(vectors):
        for f in range(fields):
            load_rows(r, f).start()
    for b in range(BLOCKS):
        for i in range(2):
            own_rows(b, i).start()

    barrier = pltpu.get_barrier_semaphore()

    def greet(k, carry):
        pl.semaphore_signal(barrier, inc=1, device_id={"tm": (me + k) % parts}, device_id_type=MESH)
        return carry

    lax.fori_loop(1, parts, greet, 0)
    pl.semaphore_signal(barrier, inc=1, device_id=across, device_id_type=MESH)
    pl.semaphore_wait(barrier, parts)

    for b in order:
        for i in range(2):
            pair_rows(b, i, other, core).start()
    for b in ring_blocks[:1]:
        for i in range(2):
            own_rows(b, i).wait()
            pair_rows(b, i, core, other).wait_recv()
    first_sends(0)
    build_choose(0, 2)
    for b in order[1:]:
        for i in range(2):
            own_rows(b, i).wait()
            pair_rows(b, i, core, other).wait_recv()
    phase(0, 0)
    first_sends(1)
    build_choose(2, 4)
    phase(0, 1)

    def order_all(r, carry):
        order_rows(r)
        pl.when(r == 0)(lambda: phase(0, 2))
        return carry

    lax.fori_loop(0, vectors, order_all, 0)
    phase(1, 0)
    phase(0, 3)

    def from_y(k, carry):
        source = chip_at(place + k)
        for i in range(2):
            over_y(i, source, 1 - group).wait_recv()
        return carry

    plan = {
        (0, 0): (lambda: phase(1, 1), lambda: first_sends(2)),
        (0, 2): (lambda: phase(1, 2),),
        (1, 0): (lambda: phase(1, 3), lambda: phase(2, 0)),
        (1, 2): (lambda: phase(2, 1),),
        (2, 0): (lambda: phase(2, 2),),
        (2, 2): (lambda: phase(2, 3),),
    }

    def after(n, slot):
        for (turn, at), acts in plan.items():
            @pl.when((n * 3 + slot) == turn * 3 + at)
            def _():
                for act in acts:
                    act()

    def job(n, carry):
        b = n + (1 - n // 2) * group * (1 - 2 * n)

        @pl.when(n == 1)
        def _():
            lax.fori_loop(1, chips, from_y, 0)

        permute(b)
        hand_over(b, core).start()
        store_moved(core, b).start()
        after(n, 0)

        def side(q, carry):
            h = core + q * (1 - 2 * core)

            @pl.when(q == 1)
            def _():
                hand_over(b, other).wait_recv()
                store_moved(other, b).start()

            to_modes(h, b)

            after(n, 1 + q)
            return carry

        lax.fori_loop(0, 2, side, 0)
        return carry

    lax.fori_loop(0, BLOCKS, job, 0)

    others(owners, lambda e: send_devs(e).start())

    def settle():
        devs_in[me] = devs[me]
        others(parts, lambda d: devs_from(d).wait_recv())
        couple()
        others(parts, lambda d: send_edges(d).start())
        edges_in[me] = edges[me]

    if_owner(settle)
    others(owners, lambda e: edges_from(e).wait_recv())
    edge_out[...] = edges_in[...]

    others(owners, lambda e: send_devs(e).wait_send())
    if_owner(lambda: others(parts, lambda d: send_edges(d).wait_send()))
    for b in order:
        for i in range(2):
            pair_rows(b, i, other, core).wait_send()
        hand_over(b, core).wait_send()
        for h in range(2):
            store_moved(h, b).wait()
            store_z(h, b).wait()
    for turn in range(3):
        def drain(s, carry):
            for d, i in BOTH:
                ring(turn, s, d, i, 0).wait_send()
            return carry

        lax.fori_loop(1, half, drain, 0)
        for d, i in LAST:
            ring(turn, half, d, i, 0).wait_send()

    def y_drain(k, carry):
        source = chip_at(place + k)
        for i in range(2):
            over_y(i, source, group).wait_send()
        return carry

    lax.fori_loop(1, chips, y_drain, 0)


def backward_kernel(z_ref, seg_ref, edge_ref, mu_ref, moved_ref, out_ref, p_ref, u_ref, back_ref):
    vectors, fields, steps, tile = out_ref.shape
    width = z_ref.shape[3]
    half_modes = BLOCKS * width
    per_seg = steps // SEGMENTS
    slabs, lanes = edge_ref.shape[2], edge_ref.shape[5]
    step = pl.program_id(0)

    def solve(h):
        root = decay_root(mu_ref[h, 0])
        root8 = tuple(jnp.broadcast_to(x, (SEGMENTS, width)) for x in root)
        jump = power(root, per_seg)
        square = mul(root, root)
        gain = mul(root, inverse_of((1.0 - square[0], -square[1])))
        perm = time_order(steps, True)
        columns = pl.ds(pl.multiple_of(h * half_modes + step * width, width), width)

        def edge(r, c):
            return jnp.concatenate([edge_ref[h, 0, j, c, pl.ds(r, 1), :] for j in range(slabs)], axis=1)

        every = range(vectors)
        p, u = [], []
        for r in every:
            row = lambda a, s: (seg_ref[h, 0, r, a, 0, s:s + 1, :], seg_ref[h, 0, r, a, 1, s:s + 1, :])
            lefts = [(edge(r, 0), edge(r, 1))]
            rights = [(edge(r, 2), edge(r, 3))]
            for s in range(SEGMENTS):
                lefts.append(add(row(0, s), mul(jump, lefts[-1])))
            for s in range(SEGMENTS - 1, 0, -1):
                rights.append(add(row(1, s), mul(jump, rights[-1])))
            rights = rights[::-1]
            ends = [mul(gain, add(rights[s], mul(root, lefts[s + 1]))) for s in range(SEGMENTS)]
            stack = lambda rows: tuple(jnp.concatenate([x[c] for x in rows], axis=0) for c in range(2))
            p.append(stack(lefts[:SEGMENTS]))
            u.append(stack(ends))
        for k in range(0, per_seg, 2):
            at = [[(r * fields + f) * steps + k * SEGMENTS for f in range(2)] for r in every]
            pair = [[z_ref[h, 0, a:a + 2 * SEGMENTS, :].astype(F32) for a in at[r]] for r in every]
            for m in range(2):
                for r in every:
                    here = tuple(x[m * SEGMENTS:(m + 1) * SEGMENTS] for x in pair[r])
                    p[r] = add(here, mul(root8, p[r]))
                    for c in range(2):
                        p_ref[r, c, pl.ds((k + m) * SEGMENTS, SEGMENTS), :] = p[r][c]
        for k in range(per_seg - 2, -1, -2):
            later = [[], []]
            for m in (1, 0):
                here = pl.ds((k + m) * SEGMENTS, SEGMENTS)
                for r in every:
                    u[r] = mul(root8, add((p_ref[r, 0, here, :], p_ref[r, 1, here, :]), u[r]))
                later[m] = list(u)
            both = pl.ds(k * SEGMENTS, 2 * SEGMENTS)
            for r in every:
                for c in range(2):
                    at = (r * fields + c) * width
                    u_ref[both, at:at + width] = jnp.concatenate(
                        [later[0][r][c], later[1][r][c]], axis=0
                    ).astype(BF16)
        turned = jnp.dot(perm, u_ref[...], preferred_element_type=F32).astype(BF16)
        for v in range(vectors * fields):
            back_ref[pl.ds(v * steps, steps), columns] = turned[:, v * width:(v + 1) * width]

    @pl.when(step < BLOCKS)
    def _():
        def one(h, carry):
            solve(h)
            return carry

        lax.fori_loop(0, 2, one, 0)

    @pl.when(step >= BLOCKS)
    def _():
        block = jnp.concatenate([moved_ref[h, b] for h in range(2) for b in range(BLOCKS)], axis=1)
        out_ref[...] = lax.dot_general(
            back_ref[...], block, (((1,), (1,)), ((), ())), preferred_element_type=F32
        ).reshape(out_ref.shape)


def on_device(residual, eigenbasis, eigenvalues, node_order):
    vectors, fields, steps, states = residual.shape
    rows, modes = eigenbasis.shape
    parts = lax.axis_size("tm")
    chips = parts // 2
    width = modes // (2 * BLOCKS)
    owners = min(parts, modes // 128)
    lanes = modes // owners
    slabs = width // lanes
    vm, anyspace = pl.BlockSpec(memory_space=pltpu.VMEM), pl.BlockSpec(memory_space=pl.ANY)
    dma = pltpu.SemaphoreType.DMA
    mu = eigenvalues.reshape(2, BLOCKS, 1, width)
    moved, z, seg, edge = pl.pallas_call(
        functools.partial(forward_kernel, chips),
        out_shape=[
            jax.ShapeDtypeStruct((2, BLOCKS, states, width), BF16),
            jax.ShapeDtypeStruct((2, BLOCKS, vectors * fields * steps, width), BF16),
            jax.ShapeDtypeStruct((2, BLOCKS, vectors, 2, 2, SEGMENTS, width), F32),
            jax.ShapeDtypeStruct((owners, 4, vectors, lanes), F32),
        ],
        in_specs=[anyspace, vm, vm, vm, anyspace],
        out_specs=[anyspace, anyspace, vm, vm],
        scratch_shapes=[
            pltpu.VMEM((BLOCKS, 2, chips, 2 * rows, width // 2), BF16),
            pltpu.VMEM((states, states), BF16),
            pltpu.VMEM((2, BLOCKS, states, width), BF16),
            pltpu.VMEM((vectors * fields * steps, states), BF16),
            pltpu.VMEM((2, BLOCKS, vectors * fields * steps, width), BF16),
            pltpu.VMEM((owners, 4, vectors, lanes), F32),
            pltpu.VMEM((parts, 4, vectors, lanes), F32),
            pltpu.VMEM((parts, 4, vectors, lanes), F32),
            pltpu.VMEM((owners, 4, vectors, lanes), F32),
            dma((8 + vectors * fields + 4 * BLOCKS,)),
            dma((8,)), dma((8,)),
            dma((12, chips // 2)), dma((12, chips // 2)),
            dma((2, chips)), dma((2, chips)),
            dma((BLOCKS,)), dma((BLOCKS,)),
            dma((owners,)), dma((parts,)), dma((parts,)), dma((owners,)),
        ],
        compiler_params=pltpu.CompilerParams(
            collective_id=0, has_side_effects=True, vmem_limit_bytes=VMEM_BYTES
        ),
        name="forward",
    )(eigenbasis, node_order.reshape(1, states), mu, eigenvalues.reshape(owners, 1, lanes), residual)

    tiles = 4
    tile = states // tiles
    solved = lambda i: jnp.minimum(i, BLOCKS - 1)
    written = lambda i: jnp.maximum(i - BLOCKS, 0)
    return pl.pallas_call(
        backward_kernel,
        grid=(BLOCKS + tiles,),
        in_specs=[
            pl.BlockSpec((2, 1, vectors * fields * steps, width), lambda i: (0, solved(i), 0, 0)),
            pl.BlockSpec((2, 1, vectors, 2, 2, SEGMENTS, width), lambda i: (0, solved(i), 0, 0, 0, 0, 0)),
            pl.BlockSpec((2, 1, slabs, 4, vectors, lanes), lambda i: (0, solved(i), 0, 0, 0, 0)),
            pl.BlockSpec((2, 1, 1, width), lambda i: (0, solved(i), 0, 0)),
            pl.BlockSpec((2, BLOCKS, tile, width), lambda i: (0, 0, written(i), 0)),
        ],
        out_specs=pl.BlockSpec((vectors, fields, steps, tile), lambda i: (0, 0, 0, written(i))),
        out_shape=jax.ShapeDtypeStruct((vectors, fields, steps, states), F32),
        scratch_shapes=[
            pltpu.VMEM((vectors, 2, steps, width), F32),
            pltpu.VMEM((steps, vectors * fields * width), BF16),
            pltpu.VMEM((vectors * fields * steps, modes), BF16),
        ],
        compiler_params=pltpu.CompilerParams(vmem_limit_bytes=VMEM_BYTES),
        name="backward",
    )(z, seg, edge.reshape(2, BLOCKS, slabs, 4, vectors, lanes), mu, moved)


def solution(mesh):
    placed = (P("grp", None, "tm", None), P("tm", None), P(), P())
    return jax.shard_map(
        on_device, mesh=mesh, in_specs=placed, out_specs=P("grp", None, "tm", None), check_vma=False
    )
```

```python
import functools

import jax
import jax.numpy as jnp
from jax import lax
from jax.experimental import pallas as pl
from jax.experimental.pallas import tpu as pltpu
from jax.sharding import PartitionSpec as P

SEGMENTS = 8
BLOCKS = 4
VMEM_BYTES = 62 * 1024 * 1024
MESH = pl.DeviceIdType.MESH
F32, BF16 = jnp.float32, jnp.bfloat16


def mul(a, b):
    return a[0] * b[0] - a[1] * b[1], a[0] * b[1] + a[1] * b[0]


def add(a, b):
    return a[0] + b[0], a[1] + b[1]


def sub(a, b):
    return a[0] - b[0], a[1] - b[1]


def inverse_of(a):
    size = a[0] * a[0] + a[1] * a[1]
    return a[0] / size, -a[1] / size


def power(a, exponent):
    result, square = None, a
    while exponent:
        if exponent & 1:
            result = square if result is None else mul(result, square)
        exponent >>= 1
        if exponent:
            square = mul(square, square)
    return result


def decay_root(mu):
    wide = 2.0 + mu
    disc_re, disc_im = wide * wide - 5.0, -2.0 * wide
    size = jnp.sqrt(disc_re * disc_re + disc_im * disc_im)
    sqrt_re = jnp.sqrt(0.5 * (size + disc_re))
    sqrt_im = 0.5 * disc_im / sqrt_re
    half = inverse_of((wide + sqrt_re, sqrt_im - 1.0))
    return 2.0 * half[0], 2.0 * half[1]


def time_order(steps, transposed):
    per_seg = steps // SEGMENTS
    row = lax.broadcasted_iota(jnp.int32, (steps, steps), 1 if transposed else 0)
    col = lax.broadcasted_iota(jnp.int32, (steps, steps), 0 if transposed else 1)
    time = (row % SEGMENTS) * per_seg + row // SEGMENTS
    return jnp.where(time == col, 1.0, 0.0).astype(BF16)


def forward_kernel(
    chips, basis_ref, node_ref, mu_ref, unit_mu_ref, residual_ref,
    moved_out, back_out,
    held, choose, moved, rows_in, z, seg, p_part, u_part, devs, devs_in, edges, edges_in,
    local_sem, pair_send, pair_recv, direct_send, direct_recv, ring_send, ring_recv, y_send, y_recv,
    block_send, block_recv, dev_send, dev_recv, edge_send, edge_recv,
):
    vectors, fields, steps, states = residual_ref.shape
    rows, modes = basis_ref.shape
    width = moved.shape[3]
    piece = width // 2
    half_modes = modes // 2
    owners, lanes = devs.shape[0], devs.shape[3]
    slabs = width // lanes
    parts = 2 * chips
    half = chips // 2
    per_seg = steps // SEGMENTS

    me, group = lax.axis_index("tm"), lax.axis_index("grp")
    core, chip = me % 2, me // 2
    other = 1 - core
    odd = chip % 2
    place = (1 - odd) * (chip // 2) + odd * (chips - 1 - chip // 2)

    def chip_at(position):
        position = (position + chips) % chips
        second = position // half
        return (1 - second) * 2 * position + second * (2 * (chips - 1 - position) + 1)

    targets = (chip_at(place + 1) * 2 + core, chip_at(place - 1) * 2 + core)
    pair = {"tm": chip * 2 + other}
    across = {"grp": 1 - group}
    order = (group, 1 - group, 2, 3)
    ring_blocks = (group, 2, 3)

    def part(r, f):
        return pl.ds(pl.multiple_of((r * fields + f) * steps, steps), steps)

    def load_rows(r, f):
        return pltpu.make_async_copy(residual_ref.at[r, f], rows_in.at[part(r, f)], local_sem.at[8 + r * fields + f])

    def own_rows(b, i):
        columns = pl.ds(pl.multiple_of(core * half_modes + b * width + i * piece, piece), piece)
        return pltpu.make_async_copy(
            basis_ref.at[:, columns], held.at[b, i, chip, pl.ds(pl.multiple_of(core * rows, rows), rows)],
            local_sem.at[b * 2 + i],
        )

    def pair_rows(b, i, side, whose):
        columns = pl.ds(pl.multiple_of(side * half_modes + b * width + i * piece, piece), piece)
        return pltpu.make_async_remote_copy(
            src_ref=basis_ref.at[:, columns],
            dst_ref=held.at[b, i, chip, pl.ds(pl.multiple_of(whose * rows, rows), rows)],
            send_sem=pair_send.at[b * 2 + i], recv_sem=pair_recv.at[b * 2 + i],
            device_id=pair, device_id_type=MESH,
        )

    def ring(turn, s, d, i, behind):
        source = chip_at(place - (s - 1 + behind)) if d == 0 else chip_at(place + (s - 1 + behind))
        ref = held.at[ring_blocks[turn], i, source]
        at = (turn * 2 + d) * 2 + i
        return pltpu.make_async_remote_copy(
            src_ref=ref, dst_ref=ref, send_sem=ring_send.at[at, s - 1], recv_sem=ring_recv.at[at, s - 1],
            device_id={"tm": targets[d]}, device_id_type=MESH,
        )

    def over_y(i, source, b):
        ref = held.at[b, i, source]
        return pltpu.make_async_remote_copy(
            src_ref=ref, dst_ref=ref, send_sem=y_send.at[i, source], recv_sem=y_recv.at[i, source],
            device_id=across, device_id_type=MESH,
        )

    BOTH = ((0, 0), (1, 0), (0, 1), (1, 1))
    LAST = ((0, 0), (1, 1))

    def direct(d, i, w, source, towards):
        columns = pl.ds(pl.multiple_of(w * half_modes + group * width + i * piece, piece), piece)
        return pltpu.make_async_remote_copy(
            src_ref=basis_ref.at[:, columns],
            dst_ref=held.at[group, i, source, pl.ds(pl.multiple_of(towards * rows, rows), rows)],
            send_sem=direct_send.at[d * 2 + i, w], recv_sem=direct_recv.at[d * 2 + i, towards],
            device_id={"tm": targets[d] - core + w}, device_id_type=MESH,
        )

    def direct_sends():
        for d, i in (BOTH if half > 1 else LAST):
            for w in range(2):
                direct(d, i, w, chip, core).start()

    def first_sends(turn):
        for d, i in (BOTH if half > 1 else LAST):
            ring(turn, 1, d, i, 0).start()

    def arrived(turn, s, d, i):
        if turn or (isinstance(s, int) and s > 1):
            ring(turn, s, d, i, 1).wait_recv()
            return
        source = chip_at(place - s) if d == 0 else chip_at(place + s)

        @pl.when(s == 1)
        def _():
            for w in range(2):
                direct(d, i, 0, source, w).wait_recv()

        @pl.when(s > 1)
        def _():
            ring(turn, s, d, i, 1).wait_recv()

    def event(turn, s, kind):
        for d, i in (LAST if kind == "last" else BOTH):
            arrived(turn, s, d, i)
            if kind == "mid" or (kind == "next_last" and i == d):
                ring(turn, s + 1, d, i, 0).start()
            if turn == 0:
                source = chip_at(place - s) if d == 0 else chip_at(place + s)
                over_y(i, source, group).start()

    def phase(turn, p):
        if p == 0:
            if half - 3 == 1:
                event(turn, 1, "mid")
            elif half > 4:
                def body(s, carry):
                    event(turn, s, "mid")
                    return carry
                lax.fori_loop(1, half - 2, body, 0)
        elif half - 3 + p >= 1:
            event(turn, half - 3 + p, ("", "mid", "next_last", "last")[p])

    def build_choose(lo, hi):
        tile = min(256, states)

        def one(t, carry):
            start = pl.multiple_of(t * tile, tile)
            index = lax.broadcasted_iota(jnp.int32, (tile, states), 0) + start
            choose[pl.ds(start, tile), :] = jnp.where(index == node_ref[...], 1.0, 0.0).astype(BF16)
            return carry

        count = states // tile
        lax.fori_loop(lo * count // 4, hi * count // 4, one, 0)

    def order_rows(r):
        tile = min(512, states)
        perm = time_order(steps, False)
        for f in range(fields):
            load_rows(r, f).wait()

        def one(t, carry):
            here = pl.ds(pl.multiple_of(t % (states // tile) * tile, tile), tile)
            rows_in[part(r, t // (states // tile)), here] = jnp.dot(
                perm, rows_in[part(r, t // (states // tile)), here], preferred_element_type=F32
            ).astype(BF16)
            return carry

        lax.fori_loop(0, fields * (states // tile), one, 0)

    def permute(b):
        tile = states // 2

        def one(t, carry):
            here = pl.ds(pl.multiple_of(t * tile, tile), tile)
            block = jnp.concatenate([held[b, i].reshape(states, piece) for i in range(2)], axis=1)
            moved[core, b, here, :] = jnp.dot(choose[here, :], block, preferred_element_type=F32).astype(BF16)
            hand_over(b, core, t).start()
            return carry

        lax.fori_loop(0, 2, one, 0)

    def hand_over(b, side, t):
        ref = moved.at[side, b, pl.ds(pl.multiple_of(t * (states // 2), states // 2), states // 2)]
        return pltpu.make_async_remote_copy(
            src_ref=ref, dst_ref=ref, send_sem=block_send.at[b, t], recv_sem=block_recv.at[b, t],
            device_id=pair, device_id_type=MESH,
        )

    def store_moved(h, b):
        return pltpu.make_async_copy(moved.at[h, b], moved_out.at[h, b], local_sem.at[8 + vectors * fields + h * BLOCKS + b])

    def store_z(h, b):
        return pltpu.make_async_copy(z.at[h, b], back_out.at[h, b], local_sem.at[8 + vectors * fields + (2 + h) * BLOCKS + b])

    def to_modes(h, b):
        root = decay_root(mu_ref[h, b])
        root8 = tuple(jnp.broadcast_to(x, (SEGMENTS, width)) for x in root)
        jump = power(root, per_seg)

        z[h, b] = jnp.dot(rows_in[...], moved[h, b], preferred_element_type=F32).astype(BF16)

        def pairs(r, k):
            at = [(r * fields + f) * steps + k * SEGMENTS for f in range(2)]
            full = [z[h, b, at[f]:at[f] + 2 * SEGMENTS, :].astype(F32) for f in range(2)]
            return [tuple(x[m * SEGMENTS:(m + 1) * SEGMENTS] for x in full) for m in range(2)]

        every = range(vectors)
        low, high = [pairs(r, 0) for r in every], [pairs(r, per_seg - 2) for r in every]
        ahead = [add(low[r][1], mul(root8, low[r][0])) for r in every]
        behind = [add(high[r][0], mul(root8, high[r][1])) for r in every]
        for k in range(2, per_seg, 2):
            low, high = [pairs(r, k) for r in every], [pairs(r, per_seg - 2 - k) for r in every]
            for m in range(2):
                ahead = [add(low[r][m], mul(root8, ahead[r])) for r in every]
                behind = [add(high[r][1 - m], mul(root8, behind[r])) for r in every]
        slab = (h * half_modes + b * width) // lanes
        row = lambda a, s: (a[0][s:s + 1], a[1][s:s + 1])
        front, back = [row(ahead[r], 0) for r in every], [row(behind[r], SEGMENTS - 1) for r in every]
        for s in range(1, SEGMENTS):
            front = [add(row(ahead[r], s), mul(jump, front[r])) for r in every]
            back = [add(row(behind[r], SEGMENTS - 1 - s), mul(jump, back[r])) for r in every]
        for r in every:
            for c in range(2):
                seg[h, b, r, 0, c] = ahead[r][c]
                seg[h, b, r, 1, c] = behind[r][c]
                for j in range(width // lanes):
                    cut = slice(j * lanes, (j + 1) * lanes)
                    devs[slab + j, c, r:r + 1, :] = front[r][c][:, cut]
                    devs[slab + j, 2 + c, r:r + 1, :] = back[r][c][:, cut]

    def send_devs(e):
        return pltpu.make_async_remote_copy(
            src_ref=devs.at[e], dst_ref=devs_in.at[me], send_sem=dev_send.at[e], recv_sem=dev_recv.at[me],
            device_id={"tm": e}, device_id_type=MESH,
        )

    def devs_from(d):
        return pltpu.make_async_remote_copy(
            src_ref=devs.at[0], dst_ref=devs_in.at[d], send_sem=dev_send.at[0], recv_sem=dev_recv.at[d],
            device_id=pair, device_id_type=MESH,
        )

    def send_edges(d):
        return pltpu.make_async_remote_copy(
            src_ref=edges.at[d], dst_ref=edges_in.at[me], send_sem=edge_send.at[d], recv_sem=edge_recv.at[me],
            device_id={"tm": d}, device_id_type=MESH,
        )

    def edges_from(e):
        return pltpu.make_async_remote_copy(
            src_ref=edges.at[0], dst_ref=edges_in.at[e], send_sem=edge_send.at[0], recv_sem=edge_recv.at[e],
            device_id=pair, device_id_type=MESH,
        )

    def others(count, act):
        def body(k, carry):
            d = (me + k) % parts
            if count == parts:
                act(d)
            else:
                pl.when(d < count)(lambda: act(d))
            return carry

        lax.fori_loop(1, parts, body, 0)

    def if_owner(act):
        if owners == parts:
            act()
        else:
            pl.when(me < owners)(act)

    def couple():
        root = decay_root(unit_mu_ref[me])
        hop = power(root, steps)
        whole = mul(power(hop, parts), root)
        square = mul(whole, whole)
        scale = mul(root, inverse_of((1.0 - square[0], -square[1])))
        zero = jnp.zeros((vectors, lanes), F32)

        def each(step, carry):
            if parts > 32:
                return lax.fori_loop(0, parts, step, carry)
            for k in range(parts):
                carry = step(k, carry)
            return carry

        def row(ref, d, c):
            return ref[d, c], ref[d, c + 1]

        def scan(k, carry):
            left, right = carry
            d = parts - 1 - k
            for c in range(2):
                edges[k, c] = left[c]
                edges[d, 2 + c] = right[c]
            return add(row(devs_in, k, 0), mul(hop, left)), add(row(devs_in, d, 2), mul(hop, right))

        all_left, all_right = each(scan, ((zero, zero), (zero, zero)))
        start_term = mul(scale, sub(all_right, mul(whole, all_left)))
        end_term = mul(scale, sub(all_left, mul(whole, all_right)))

        def correct(k, carry):
            start_term, end_term = carry
            d = parts - 1 - k
            left, right = sub(row(edges, k, 0), start_term), sub(row(edges, d, 2), end_term)
            for c in range(2):
                edges[k, c] = left[c]
                edges[d, 2 + c] = right[c]
            return mul(hop, start_term), mul(hop, end_term)

        each(correct, (start_term, end_term))

    def solve(h, b):
        root = decay_root(mu_ref[h, b])
        root8 = tuple(jnp.broadcast_to(x, (SEGMENTS, width)) for x in root)
        jump = power(root, per_seg)
        square = mul(root, root)
        gain = mul(root, inverse_of((1.0 - square[0], -square[1])))
        perm = time_order(steps, True)
        slab = (h * half_modes + b * width) // lanes

        def edge(r, c):
            return jnp.concatenate([edges_in[slab + j, c, r:r + 1, :] for j in range(width // lanes)], axis=1)

        every = range(vectors)
        p, u = [], []
        for r in every:
            row = lambda a, s: (seg[h, b, r, a, 0, s:s + 1, :], seg[h, b, r, a, 1, s:s + 1, :])
            lefts = [(edge(r, 0), edge(r, 1))]
            rights = [(edge(r, 2), edge(r, 3))]
            for s in range(SEGMENTS):
                lefts.append(add(row(0, s), mul(jump, lefts[-1])))
            for s in range(SEGMENTS - 1, 0, -1):
                rights.append(add(row(1, s), mul(jump, rights[-1])))
            rights = rights[::-1]
            ends = [mul(gain, add(rights[s], mul(root, lefts[s + 1]))) for s in range(SEGMENTS)]
            stack = lambda rows: tuple(jnp.concatenate([x[c] for x in rows], axis=0) for c in range(2))
            p.append(stack(lefts[:SEGMENTS]))
            u.append(stack(ends))
        for k in range(0, per_seg, 2):
            at = [[(r * fields + f) * steps + k * SEGMENTS for f in range(2)] for r in every]
            pair = [[z[h, b, a:a + 2 * SEGMENTS, :].astype(F32) for a in at[r]] for r in every]
            for m in range(2):
                for r in every:
                    here = tuple(x[m * SEGMENTS:(m + 1) * SEGMENTS] for x in pair[r])
                    p[r] = add(here, mul(root8, p[r]))
                    for c in range(2):
                        p_part[r, c, pl.ds((k + m) * SEGMENTS, SEGMENTS), :] = p[r][c]
        for k in range(per_seg - 2, -1, -2):
            later = [[], []]
            for m in (1, 0):
                here = pl.ds((k + m) * SEGMENTS, SEGMENTS)
                for r in every:
                    u[r] = mul(root8, add((p_part[r, 0, here, :], p_part[r, 1, here, :]), u[r]))
                later[m] = list(u)
            both = pl.ds(k * SEGMENTS, 2 * SEGMENTS)
            for r in every:
                for c in range(2):
                    at = (r * fields + c) * width
                    u_part[both, at:at + width] = jnp.concatenate(
                        [later[0][r][c], later[1][r][c]], axis=0
                    ).astype(BF16)
        turned = jnp.dot(perm, u_part[...], preferred_element_type=F32).astype(BF16)
        for v in range(vectors * fields):
            z[h, b, v * steps:(v + 1) * steps, :] = turned[:, v * width:(v + 1) * width]

    for r in range(vectors):
        for f in range(fields):
            load_rows(r, f).start()
    for b in range(BLOCKS):
        for i in range(2):
            own_rows(b, i).start()

    barrier = pltpu.get_barrier_semaphore()

    def greet(k, carry):
        pl.semaphore_signal(barrier, inc=1, device_id={"tm": (me + k) % parts}, device_id_type=MESH)
        return carry

    lax.fori_loop(1, parts, greet, 0)
    pl.semaphore_signal(barrier, inc=1, device_id=across, device_id_type=MESH)
    pl.semaphore_wait(barrier, parts)

    direct_sends()
    for b in order:
        for i in range(2):
            pair_rows(b, i, other, core).start()
    build_choose(0, 2)
    for b in order:
        for i in range(2):
            own_rows(b, i).wait()
            pair_rows(b, i, core, other).wait_recv()
    phase(0, 0)
    first_sends(1)
    build_choose(2, 4)
    phase(0, 1)

    def order_all(r, carry):
        order_rows(r)
        pl.when(r == 0)(lambda: phase(0, 2))
        return carry

    lax.fori_loop(0, vectors, order_all, 0)
    phase(1, 0)
    phase(0, 3)

    def from_y(k, carry):
        source = chip_at(place + k)
        for i in range(2):
            over_y(i, source, 1 - group).wait_recv()
        return carry

    plan = {
        (0, 0): (lambda: phase(1, 1), lambda: first_sends(2)),
        (0, 2): (lambda: phase(1, 2),),
        (1, 0): (lambda: phase(1, 3), lambda: phase(2, 0)),
        (1, 2): (lambda: phase(2, 1),),
        (2, 0): (lambda: phase(2, 2),),
        (2, 2): (lambda: phase(2, 3),),
    }

    def after(n, slot):
        for (turn, at), acts in plan.items():
            @pl.when((n * 3 + slot) == turn * 3 + at)
            def _():
                for act in acts:
                    act()

    def block_at(n):
        return n + (1 - n // 2) * group * (1 - 2 * n)

    def each_slab(b, act):
        def body(q, carry):
            e = ((q // slabs) * half_modes + b * width) // lanes + q % slabs
            pl.when(e != me)(lambda: act(e))
            return carry

        lax.fori_loop(0, 2 * slabs, body, 0)

    def settle(b):
        @pl.when((me < owners) & ((me * lanes) % half_modes // width == b))
        def _():
            devs_in[me] = devs[me]
            others(parts, lambda d: devs_from(d).wait_recv())
            couple()
            others(parts, lambda d: send_edges(d).start())
            edges_in[me] = edges[me]

    def finish(b):
        each_slab(b, lambda e: edges_from(e).wait_recv())

        def one(h, carry):
            solve(h, b)
            store_z(h, b).start()
            return carry

        lax.fori_loop(0, 2, one, 0)

    def job(n, carry):
        b, last = block_at(n), block_at(n - 1)

        @pl.when(n < BLOCKS)
        def _():
            @pl.when(n == 1)
            def _():
                lax.fori_loop(1, chips, from_y, 0)

            permute(b)
            store_moved(core, b).start()
            after(n, 0)

        @pl.when(n > 0)
        def _():
            settle(last)

        @pl.when(n < BLOCKS)
        def _():
            def side(q, carry):
                h = core + q * (1 - 2 * core)

                @pl.when(q == 1)
                def _():
                    for t in range(2):
                        hand_over(b, other, t).wait_recv()
                    store_moved(other, b).start()

                to_modes(h, b)
                pl.when(q == 1)(lambda: each_slab(b, lambda e: send_devs(e).start()))
                after(n, 1 + q)
                return carry

            lax.fori_loop(0, 2, side, 0)

        @pl.when(n > 0)
        def _():
            finish(last)

        return carry

    lax.fori_loop(0, BLOCKS + 1, job, 0)

    others(owners, lambda e: send_devs(e).wait_send())
    if_owner(lambda: others(parts, lambda d: send_edges(d).wait_send()))
    for b in order:
        for i in range(2):
            pair_rows(b, i, other, core).wait_send()
        for t in range(2):
            hand_over(b, core, t).wait_send()
        for h in range(2):
            store_moved(h, b).wait()
            store_z(h, b).wait()
    for turn in range(3):
        def drain(s, carry):
            for d, i in BOTH:
                ring(turn, s, d, i, 0).wait_send()
            return carry

        lax.fori_loop(1 if turn else 2, half, drain, 0)
        if turn or half > 1:
            for d, i in LAST:
                ring(turn, half, d, i, 0).wait_send()
    for d, i in (BOTH if half > 1 else LAST):
        for w in range(2):
            direct(d, i, w, chip, core).wait_send()

    def y_drain(k, carry):
        source = chip_at(place + k)
        for i in range(2):
            over_y(i, source, group).wait_send()
        return carry

    lax.fori_loop(1, chips, y_drain, 0)


def backward_kernel(back_ref, moved_ref, out_ref):
    halves = [(h, b) for h in range(2) for b in range(BLOCKS)]
    back = jnp.concatenate([back_ref[h, b] for h, b in halves], axis=1)
    block = jnp.concatenate([moved_ref[h, b] for h, b in halves], axis=1)
    out_ref[...] = lax.dot_general(
        back, block, (((1,), (1,)), ((), ())), preferred_element_type=F32
    ).reshape(out_ref.shape)


def on_device(residual, eigenbasis, eigenvalues, node_order):
    vectors, fields, steps, states = residual.shape
    rows, modes = eigenbasis.shape
    parts = lax.axis_size("tm")
    chips = parts // 2
    width = modes // (2 * BLOCKS)
    owners = min(parts, modes // 128)
    lanes = modes // owners
    vm, anyspace = pl.BlockSpec(memory_space=pltpu.VMEM), pl.BlockSpec(memory_space=pl.ANY)
    dma = pltpu.SemaphoreType.DMA
    mu = eigenvalues.reshape(2, BLOCKS, 1, width)
    moved, back = pl.pallas_call(
        functools.partial(forward_kernel, chips),
        out_shape=[
            jax.ShapeDtypeStruct((2, BLOCKS, states, width), BF16),
            jax.ShapeDtypeStruct((2, BLOCKS, vectors * fields * steps, width), BF16),
        ],
        in_specs=[anyspace, vm, vm, vm, anyspace],
        out_specs=[anyspace, anyspace],
        scratch_shapes=[
            pltpu.VMEM((BLOCKS, 2, chips, 2 * rows, width // 2), BF16),
            pltpu.VMEM((states, states), BF16),
            pltpu.VMEM((2, BLOCKS, states, width), BF16),
            pltpu.VMEM((vectors * fields * steps, states), BF16),
            pltpu.VMEM((2, BLOCKS, vectors * fields * steps, width), BF16),
            pltpu.VMEM((2, BLOCKS, vectors, 2, 2, SEGMENTS, width), F32),
            pltpu.VMEM((vectors, 2, steps, width), F32),
            pltpu.VMEM((steps, vectors * fields * width), BF16),
            pltpu.VMEM((owners, 4, vectors, lanes), F32),
            pltpu.VMEM((parts, 4, vectors, lanes), F32),
            pltpu.VMEM((parts, 4, vectors, lanes), F32),
            pltpu.VMEM((owners, 4, vectors, lanes), F32),
            dma((8 + vectors * fields + 4 * BLOCKS,)),
            dma((8,)), dma((8,)),
            dma((4, 2)), dma((4, 2)),
            dma((12, chips // 2)), dma((12, chips // 2)),
            dma((2, chips)), dma((2, chips)),
            dma((BLOCKS, 2)), dma((BLOCKS, 2)),
            dma((owners,)), dma((parts,)), dma((parts,)), dma((owners,)),
        ],
        compiler_params=pltpu.CompilerParams(
            collective_id=0, has_side_effects=True, vmem_limit_bytes=VMEM_BYTES
        ),
        name="forward",
    )(eigenbasis, node_order.reshape(1, states), mu, eigenvalues.reshape(owners, 1, lanes), residual)

    tiles = 4
    tile = states // tiles
    return pl.pallas_call(
        backward_kernel,
        grid=(tiles,),
        in_specs=[
            pl.BlockSpec((2, BLOCKS, vectors * fields * steps, width), lambda i: (0, 0, 0, 0)),
            pl.BlockSpec((2, BLOCKS, tile, width), lambda i: (0, 0, i, 0)),
        ],
        out_specs=pl.BlockSpec((vectors, fields, steps, tile), lambda i: (0, 0, 0, i)),
        out_shape=jax.ShapeDtypeStruct((vectors, fields, steps, states), F32),
        compiler_params=pltpu.CompilerParams(vmem_limit_bytes=VMEM_BYTES),
        name="backward",
    )(back, moved)


def solution(mesh):
    placed = (P("grp", None, "tm", None), P("tm", None), P(), P())
    return jax.shard_map(
        on_device, mesh=mesh, in_specs=placed, out_specs=P("grp", None, "tm", None), check_vma=False
    )
```

```python
import functools

import jax
import jax.numpy as jnp
from jax import lax
from jax.experimental import pallas as pl
from jax.experimental.pallas import tpu as pltpu
from jax.sharding import PartitionSpec as P

SEGMENTS = 8
BLOCKS = 4
VMEM_BYTES = 62 * 1024 * 1024
MESH = pl.DeviceIdType.MESH
F32, BF16 = jnp.float32, jnp.bfloat16


def mul(a, b):
    return a[0] * b[0] - a[1] * b[1], a[0] * b[1] + a[1] * b[0]


def add(a, b):
    return a[0] + b[0], a[1] + b[1]


def sub(a, b):
    return a[0] - b[0], a[1] - b[1]


def inverse_of(a):
    size = a[0] * a[0] + a[1] * a[1]
    return a[0] / size, -a[1] / size


def power(a, exponent):
    result, square = None, a
    while exponent:
        if exponent & 1:
            result = square if result is None else mul(result, square)
        exponent >>= 1
        if exponent:
            square = mul(square, square)
    return result


def decay_root(mu):
    wide = 2.0 + mu
    disc_re, disc_im = wide * wide - 5.0, -2.0 * wide
    size = jnp.sqrt(disc_re * disc_re + disc_im * disc_im)
    sqrt_re = jnp.sqrt(0.5 * (size + disc_re))
    sqrt_im = 0.5 * disc_im / sqrt_re
    half = inverse_of((wide + sqrt_re, sqrt_im - 1.0))
    return 2.0 * half[0], 2.0 * half[1]


def time_order(steps, transposed):
    per_seg = steps // SEGMENTS
    row = lax.broadcasted_iota(jnp.int32, (steps, steps), 1 if transposed else 0)
    col = lax.broadcasted_iota(jnp.int32, (steps, steps), 0 if transposed else 1)
    time = (row % SEGMENTS) * per_seg + row // SEGMENTS
    return jnp.where(time == col, 1.0, 0.0).astype(BF16)


def forward_kernel(
    chips, basis_ref, node_ref, mu_ref, unit_mu_ref, residual_ref,
    moved_out, back_out,
    held, choose, moved, rows_in, z, seg, p_part, u_part, devs, devs_in, edges, edges_in,
    local_sem, pair_send, pair_recv, direct_send, direct_recv, ring_send, ring_recv, y_send, y_recv,
    block_send, block_recv, dev_send, dev_recv, edge_send, edge_recv,
):
    vectors, fields, steps, states = residual_ref.shape
    rows, modes = basis_ref.shape
    width = moved.shape[3]
    piece = width // 2
    half_modes = modes // 2
    owners, lanes = devs.shape[0], devs.shape[3]
    slabs = width // lanes
    parts = 2 * chips
    half = chips // 2
    per_seg = steps // SEGMENTS

    me, group = lax.axis_index("tm"), lax.axis_index("grp")
    core, chip = me % 2, me // 2
    other = 1 - core
    odd = chip % 2
    place = (1 - odd) * (chip // 2) + odd * (chips - 1 - chip // 2)

    def chip_at(position):
        position = (position + chips) % chips
        second = position // half
        return (1 - second) * 2 * position + second * (2 * (chips - 1 - position) + 1)

    targets = (chip_at(place + 1) * 2 + core, chip_at(place - 1) * 2 + core)
    pair = {"tm": chip * 2 + other}
    across = {"grp": 1 - group}
    order = (group, 1 - group, 2, 3)
    ring_blocks = (group, 2, 3)

    def part(r, f):
        return pl.ds(pl.multiple_of((r * fields + f) * steps, steps), steps)

    def load_rows(r, f):
        return pltpu.make_async_copy(residual_ref.at[r, f], rows_in.at[part(r, f)], local_sem.at[8 + r * fields + f])

    def own_rows(b, i):
        columns = pl.ds(pl.multiple_of(core * half_modes + b * width + i * piece, piece), piece)
        return pltpu.make_async_copy(
            basis_ref.at[:, columns], held.at[b, i, chip, pl.ds(pl.multiple_of(core * rows, rows), rows)],
            local_sem.at[b * 2 + i],
        )

    def pair_rows(b, i, side, whose):
        columns = pl.ds(pl.multiple_of(side * half_modes + b * width + i * piece, piece), piece)
        return pltpu.make_async_remote_copy(
            src_ref=basis_ref.at[:, columns],
            dst_ref=held.at[b, i, chip, pl.ds(pl.multiple_of(whose * rows, rows), rows)],
            send_sem=pair_send.at[b * 2 + i], recv_sem=pair_recv.at[b * 2 + i],
            device_id=pair, device_id_type=MESH,
        )

    def ring(turn, s, d, i, behind):
        source = chip_at(place - (s - 1 + behind)) if d == 0 else chip_at(place + (s - 1 + behind))
        ref = held.at[ring_blocks[turn], i, source]
        at = (turn * 2 + d) * 2 + i
        return pltpu.make_async_remote_copy(
            src_ref=ref, dst_ref=ref, send_sem=ring_send.at[at, s - 1], recv_sem=ring_recv.at[at, s - 1],
            device_id={"tm": targets[d]}, device_id_type=MESH,
        )

    def over_y(i, source, b):
        ref = held.at[b, i, source]
        return pltpu.make_async_remote_copy(
            src_ref=ref, dst_ref=ref, send_sem=y_send.at[i, source], recv_sem=y_recv.at[i, source],
            device_id=across, device_id_type=MESH,
        )

    BOTH = ((0, 0), (1, 0), (0, 1), (1, 1))
    LAST = ((0, 0), (1, 1))

    def direct(d, i, w, source, towards):
        columns = pl.ds(pl.multiple_of(w * half_modes + group * width + i * piece, piece), piece)
        return pltpu.make_async_remote_copy(
            src_ref=basis_ref.at[:, columns],
            dst_ref=held.at[group, i, source, pl.ds(pl.multiple_of(towards * rows, rows), rows)],
            send_sem=direct_send.at[d * 2 + i, w], recv_sem=direct_recv.at[d * 2 + i, towards],
            device_id={"tm": targets[d] - core + w}, device_id_type=MESH,
        )

    def direct_sends():
        for d, i in (BOTH if half > 1 else LAST):
            for w in range(2):
                direct(d, i, w, chip, core).start()

    def first_sends(turn):
        for d, i in (BOTH if half > 1 else LAST):
            ring(turn, 1, d, i, 0).start()

    def arrived(turn, s, d, i):
        if turn or (isinstance(s, int) and s > 1):
            ring(turn, s, d, i, 1).wait_recv()
            return
        source = chip_at(place - s) if d == 0 else chip_at(place + s)

        @pl.when(s == 1)
        def _():
            for w in range(2):
                direct(d, i, 0, source, w).wait_recv()

        @pl.when(s > 1)
        def _():
            ring(turn, s, d, i, 1).wait_recv()

    def event(turn, s, kind):
        for d, i in (LAST if kind == "last" else BOTH):
            arrived(turn, s, d, i)
            if kind == "mid" or (kind == "next_last" and i == d):
                ring(turn, s + 1, d, i, 0).start()
            if turn == 0:
                source = chip_at(place - s) if d == 0 else chip_at(place + s)
                over_y(i, source, group).start()

    def phase(turn, p):
        if p == 0:
            if half - 3 == 1:
                event(turn, 1, "mid")
            elif half > 4:
                def body(s, carry):
                    event(turn, s, "mid")
                    return carry
                lax.fori_loop(1, half - 2, body, 0)
        elif half - 3 + p >= 1:
            event(turn, half - 3 + p, ("", "mid", "next_last", "last")[p])

    def build_choose(lo, hi):
        tile = min(256, states)

        def one(t, carry):
            start = pl.multiple_of(t * tile, tile)
            index = lax.broadcasted_iota(jnp.int32, (tile, states), 0) + start
            choose[pl.ds(start, tile), :] = jnp.where(index == node_ref[...], 1.0, 0.0).astype(BF16)
            return carry

        count = states // tile
        lax.fori_loop(lo * count // 4, hi * count // 4, one, 0)

    def order_rows(r):
        tile = min(512, states)
        perm = time_order(steps, False)
        for f in range(fields):
            load_rows(r, f).wait()

        def one(t, carry):
            here = pl.ds(pl.multiple_of(t % (states // tile) * tile, tile), tile)
            rows_in[part(r, t // (states // tile)), here] = jnp.dot(
                perm, rows_in[part(r, t // (states // tile)), here], preferred_element_type=F32
            ).astype(BF16)
            return carry

        lax.fori_loop(0, fields * (states // tile), one, 0)

    def permute(b):
        tile = states // 2

        def one(t, carry):
            here = pl.ds(pl.multiple_of(t * tile, tile), tile)
            block = jnp.concatenate([held[b, i].reshape(states, piece) for i in range(2)], axis=1)
            moved[core, b, here, :] = jnp.dot(choose[here, :], block, preferred_element_type=F32).astype(BF16)
            hand_over(b, core, t).start()
            return carry

        lax.fori_loop(0, 2, one, 0)

    def hand_over(b, side, t):
        ref = moved.at[side, b, pl.ds(pl.multiple_of(t * (states // 2), states // 2), states // 2)]
        return pltpu.make_async_remote_copy(
            src_ref=ref, dst_ref=ref, send_sem=block_send.at[b, t], recv_sem=block_recv.at[b, t],
            device_id=pair, device_id_type=MESH,
        )

    def store_moved(h, b):
        return pltpu.make_async_copy(moved.at[h, b], moved_out.at[h, b], local_sem.at[8 + vectors * fields + h * BLOCKS + b])

    def store_z(h, b):
        return pltpu.make_async_copy(z.at[h, b], back_out.at[h, b], local_sem.at[8 + vectors * fields + (2 + h) * BLOCKS + b])

    def to_modes(h, b):
        root = decay_root(mu_ref[h, b])
        root8 = tuple(jnp.broadcast_to(x, (SEGMENTS, width)) for x in root)
        jump = power(root, per_seg)

        z[h, b] = jnp.dot(rows_in[...], moved[h, b], preferred_element_type=F32).astype(BF16)

        def pairs(r, k):
            at = [(r * fields + f) * steps + k * SEGMENTS for f in range(2)]
            full = [z[h, b, at[f]:at[f] + 2 * SEGMENTS, :].astype(F32) for f in range(2)]
            return [tuple(x[m * SEGMENTS:(m + 1) * SEGMENTS] for x in full) for m in range(2)]

        every = range(vectors)
        low, high = [pairs(r, 0) for r in every], [pairs(r, per_seg - 2) for r in every]
        ahead = [add(low[r][1], mul(root8, low[r][0])) for r in every]
        behind = [add(high[r][0], mul(root8, high[r][1])) for r in every]
        for k in range(2, per_seg, 2):
            low, high = [pairs(r, k) for r in every], [pairs(r, per_seg - 2 - k) for r in every]
            for m in range(2):
                ahead = [add(low[r][m], mul(root8, ahead[r])) for r in every]
                behind = [add(high[r][1 - m], mul(root8, behind[r])) for r in every]
        slab = (h * half_modes + b * width) // lanes
        row = lambda a, s: (a[0][s:s + 1], a[1][s:s + 1])
        front, back = [row(ahead[r], 0) for r in every], [row(behind[r], SEGMENTS - 1) for r in every]
        for s in range(1, SEGMENTS):
            front = [add(row(ahead[r], s), mul(jump, front[r])) for r in every]
            back = [add(row(behind[r], SEGMENTS - 1 - s), mul(jump, back[r])) for r in every]
        for r in every:
            for c in range(2):
                seg[h, b, r, 0, c] = ahead[r][c]
                seg[h, b, r, 1, c] = behind[r][c]
                for j in range(width // lanes):
                    cut = slice(j * lanes, (j + 1) * lanes)
                    devs[slab + j, c, r:r + 1, :] = front[r][c][:, cut]
                    devs[slab + j, 2 + c, r:r + 1, :] = back[r][c][:, cut]

    def send_devs(e):
        return pltpu.make_async_remote_copy(
            src_ref=devs.at[e], dst_ref=devs_in.at[me], send_sem=dev_send.at[e], recv_sem=dev_recv.at[me],
            device_id={"tm": e}, device_id_type=MESH,
        )

    def devs_from(d):
        return pltpu.make_async_remote_copy(
            src_ref=devs.at[0], dst_ref=devs_in.at[d], send_sem=dev_send.at[0], recv_sem=dev_recv.at[d],
            device_id=pair, device_id_type=MESH,
        )

    def send_edges(d):
        return pltpu.make_async_remote_copy(
            src_ref=edges.at[d], dst_ref=edges_in.at[me], send_sem=edge_send.at[d], recv_sem=edge_recv.at[me],
            device_id={"tm": d}, device_id_type=MESH,
        )

    def edges_from(e):
        return pltpu.make_async_remote_copy(
            src_ref=edges.at[0], dst_ref=edges_in.at[e], send_sem=edge_send.at[0], recv_sem=edge_recv.at[e],
            device_id=pair, device_id_type=MESH,
        )

    def others(count, act):
        def body(k, carry):
            d = (me + k) % parts
            if count == parts:
                act(d)
            else:
                pl.when(d < count)(lambda: act(d))
            return carry

        lax.fori_loop(1, parts, body, 0)

    def if_owner(act):
        if owners == parts:
            act()
        else:
            pl.when(me < owners)(act)

    def couple():
        root = decay_root(unit_mu_ref[me])
        hop = power(root, steps)
        whole = mul(power(hop, parts), root)
        square = mul(whole, whole)
        scale = mul(root, inverse_of((1.0 - square[0], -square[1])))
        zero = jnp.zeros((vectors, lanes), F32)

        def each(step, carry):
            if parts > 32:
                return lax.fori_loop(0, parts, step, carry)
            for k in range(parts):
                carry = step(k, carry)
            return carry

        def row(ref, d, c):
            return ref[d, c], ref[d, c + 1]

        def scan(k, carry):
            left, right = carry
            d = parts - 1 - k
            for c in range(2):
                edges[k, c] = left[c]
                edges[d, 2 + c] = right[c]
            return add(row(devs_in, k, 0), mul(hop, left)), add(row(devs_in, d, 2), mul(hop, right))

        all_left, all_right = each(scan, ((zero, zero), (zero, zero)))
        start_term = mul(scale, sub(all_right, mul(whole, all_left)))
        end_term = mul(scale, sub(all_left, mul(whole, all_right)))

        def correct(k, carry):
            start_term, end_term = carry
            d = parts - 1 - k
            left, right = sub(row(edges, k, 0), start_term), sub(row(edges, d, 2), end_term)
            for c in range(2):
                edges[k, c] = left[c]
                edges[d, 2 + c] = right[c]
            return mul(hop, start_term), mul(hop, end_term)

        each(correct, (start_term, end_term))

    def solve(h, b):
        root = decay_root(mu_ref[h, b])
        root8 = tuple(jnp.broadcast_to(x, (SEGMENTS, width)) for x in root)
        jump = power(root, per_seg)
        square = mul(root, root)
        gain = mul(root, inverse_of((1.0 - square[0], -square[1])))
        perm = time_order(steps, True)
        slab = (h * half_modes + b * width) // lanes

        def edge(r, c):
            return jnp.concatenate([edges_in[slab + j, c, r:r + 1, :] for j in range(width // lanes)], axis=1)

        every = range(vectors)
        p, u = [], []
        for r in every:
            row = lambda a, s: (seg[h, b, r, a, 0, s:s + 1, :], seg[h, b, r, a, 1, s:s + 1, :])
            lefts = [(edge(r, 0), edge(r, 1))]
            rights = [(edge(r, 2), edge(r, 3))]
            for s in range(SEGMENTS):
                lefts.append(add(row(0, s), mul(jump, lefts[-1])))
            for s in range(SEGMENTS - 1, 0, -1):
                rights.append(add(row(1, s), mul(jump, rights[-1])))
            rights = rights[::-1]
            ends = [mul(gain, add(rights[s], mul(root, lefts[s + 1]))) for s in range(SEGMENTS)]
            stack = lambda rows: tuple(jnp.concatenate([x[c] for x in rows], axis=0) for c in range(2))
            p.append(stack(lefts[:SEGMENTS]))
            u.append(stack(ends))
        for k in range(0, per_seg, 2):
            at = [[(r * fields + f) * steps + k * SEGMENTS for f in range(2)] for r in every]
            pair = [[z[h, b, a:a + 2 * SEGMENTS, :].astype(F32) for a in at[r]] for r in every]
            for m in range(2):
                for r in every:
                    here = tuple(x[m * SEGMENTS:(m + 1) * SEGMENTS] for x in pair[r])
                    p[r] = add(here, mul(root8, p[r]))
                    for c in range(2):
                        p_part[r, c, pl.ds((k + m) * SEGMENTS, SEGMENTS), :] = p[r][c]
        for k in range(per_seg - 2, -1, -2):
            later = [[], []]
            for m in (1, 0):
                here = pl.ds((k + m) * SEGMENTS, SEGMENTS)
                for r in every:
                    u[r] = mul(root8, add((p_part[r, 0, here, :], p_part[r, 1, here, :]), u[r]))
                later[m] = list(u)
            both = pl.ds(k * SEGMENTS, 2 * SEGMENTS)
            for r in every:
                for c in range(2):
                    at = (r * fields + c) * width
                    u_part[both, at:at + width] = jnp.concatenate(
                        [later[0][r][c], later[1][r][c]], axis=0
                    ).astype(BF16)
        turned = jnp.dot(perm, u_part[...], preferred_element_type=F32).astype(BF16)
        for v in range(vectors * fields):
            z[h, b, v * steps:(v + 1) * steps, :] = turned[:, v * width:(v + 1) * width]

    for r in range(vectors):
        for f in range(fields):
            load_rows(r, f).start()
    for b in range(BLOCKS):
        for i in range(2):
            own_rows(b, i).start()

    barrier = pltpu.get_barrier_semaphore()

    def greet(k, carry):
        pl.semaphore_signal(barrier, inc=1, device_id={"tm": (me + k) % parts}, device_id_type=MESH)
        return carry

    lax.fori_loop(1, parts, greet, 0)
    pl.semaphore_signal(barrier, inc=1, device_id=across, device_id_type=MESH)
    pl.semaphore_wait(barrier, parts)

    direct_sends()
    for b in order:
        for i in range(2):
            pair_rows(b, i, other, core).start()
    build_choose(0, 2)
    for b in order:
        for i in range(2):
            own_rows(b, i).wait()
            pair_rows(b, i, core, other).wait_recv()
    phase(0, 0)
    first_sends(1)
    build_choose(2, 4)
    phase(0, 1)

    def order_all(r, carry):
        order_rows(r)
        pl.when(r == 0)(lambda: phase(0, 2))
        return carry

    lax.fori_loop(0, vectors, order_all, 0)
    phase(1, 0)
    phase(0, 3)

    def from_y(k, carry):
        source = chip_at(place + k)
        for i in range(2):
            over_y(i, source, 1 - group).wait_recv()
        return carry

    plan = {
        (0, 0): (lambda: phase(1, 1), lambda: first_sends(2)),
        (0, 2): (lambda: phase(1, 2),),
        (1, 0): (lambda: phase(1, 3), lambda: phase(2, 0)),
        (1, 2): (lambda: phase(2, 1),),
        (2, 0): (lambda: phase(2, 2),),
        (2, 2): (lambda: phase(2, 3),),
    }

    def after(n, slot):
        for (turn, at), acts in plan.items():
            @pl.when((n * 3 + slot) == turn * 3 + at)
            def _():
                for act in acts:
                    act()

    def block_at(n):
        return n + (1 - n // 2) * group * (1 - 2 * n)

    def each_slab(b, act):
        def body(q, carry):
            e = ((q // slabs) * half_modes + b * width) // lanes + q % slabs
            pl.when(e != me)(lambda: act(e))
            return carry

        lax.fori_loop(0, 2 * slabs, body, 0)

    def settle(b):
        @pl.when((me < owners) & ((me * lanes) % half_modes // width == b))
        def _():
            devs_in[me] = devs[me]
            others(parts, lambda d: devs_from(d).wait_recv())
            couple()
            others(parts, lambda d: send_edges(d).start())
            edges_in[me] = edges[me]

    def finish(b):
        each_slab(b, lambda e: edges_from(e).wait_recv())

        def one(h, carry):
            solve(h, b)
            store_z(h, b).start()
            return carry

        lax.fori_loop(0, 2, one, 0)

    def job(n, carry):
        b, last = block_at(n), block_at(n - 1)

        @pl.when(n == 1)
        def _():
            lax.fori_loop(1, chips, from_y, 0)

        permute(b)
        store_moved(core, b).start()
        after(n, 0)

        def side(q, carry):
            h = core + q * (1 - 2 * core)

            @pl.when(q == 1)
            def _():
                for t in range(2):
                    hand_over(b, other, t).wait_recv()
                store_moved(other, b).start()

            to_modes(h, b)
            pl.when(q == 1)(lambda: each_slab(b, lambda e: send_devs(e).start()))
            after(n, 1 + q)
            return carry

        lax.fori_loop(0, 2, side, 0)

        @pl.when(n > 0)
        def _():
            settle(last)

        return carry

    lax.fori_loop(0, BLOCKS, job, 0)

    def tail(m, carry):
        pl.when(m == 2)(lambda: settle(block_at(BLOCKS - 1)))
        finish(block_at(m))
        return carry

    lax.fori_loop(0, BLOCKS, tail, 0)

    others(owners, lambda e: send_devs(e).wait_send())
    if_owner(lambda: others(parts, lambda d: send_edges(d).wait_send()))
    for b in order:
        for i in range(2):
            pair_rows(b, i, other, core).wait_send()
        for t in range(2):
            hand_over(b, core, t).wait_send()
        for h in range(2):
            store_moved(h, b).wait()
            store_z(h, b).wait()
    for turn in range(3):
        def drain(s, carry):
            for d, i in BOTH:
                ring(turn, s, d, i, 0).wait_send()
            return carry

        lax.fori_loop(1 if turn else 2, half, drain, 0)
        if turn or half > 1:
            for d, i in LAST:
                ring(turn, half, d, i, 0).wait_send()
    for d, i in (BOTH if half > 1 else LAST):
        for w in range(2):
            direct(d, i, w, chip, core).wait_send()

    def y_drain(k, carry):
        source = chip_at(place + k)
        for i in range(2):
            over_y(i, source, group).wait_send()
        return carry

    lax.fori_loop(1, chips, y_drain, 0)


def backward_kernel(back_ref, moved_ref, out_ref):
    halves = [(h, b) for h in range(2) for b in range(BLOCKS)]
    back = jnp.concatenate([back_ref[h, b] for h, b in halves], axis=1)
    block = jnp.concatenate([moved_ref[h, b] for h, b in halves], axis=1)
    out_ref[...] = lax.dot_general(
        back, block, (((1,), (1,)), ((), ())), preferred_element_type=F32
    ).reshape(out_ref.shape)


def on_device(residual, eigenbasis, eigenvalues, node_order):
    vectors, fields, steps, states = residual.shape
    rows, modes = eigenbasis.shape
    parts = lax.axis_size("tm")
    chips = parts // 2
    width = modes // (2 * BLOCKS)
    owners = min(parts, modes // 128)
    lanes = modes // owners
    vm, anyspace = pl.BlockSpec(memory_space=pltpu.VMEM), pl.BlockSpec(memory_space=pl.ANY)
    dma = pltpu.SemaphoreType.DMA
    mu = eigenvalues.reshape(2, BLOCKS, 1, width)
    moved, back = pl.pallas_call(
        functools.partial(forward_kernel, chips),
        out_shape=[
            jax.ShapeDtypeStruct((2, BLOCKS, states, width), BF16),
            jax.ShapeDtypeStruct((2, BLOCKS, vectors * fields * steps, width), BF16),
        ],
        in_specs=[anyspace, vm, vm, vm, anyspace],
        out_specs=[anyspace, anyspace],
        scratch_shapes=[
            pltpu.VMEM((BLOCKS, 2, chips, 2 * rows, width // 2), BF16),
            pltpu.VMEM((states, states), BF16),
            pltpu.VMEM((2, BLOCKS, states, width), BF16),
            pltpu.VMEM((vectors * fields * steps, states), BF16),
            pltpu.VMEM((2, BLOCKS, vectors * fields * steps, width), BF16),
            pltpu.VMEM((2, BLOCKS, vectors, 2, 2, SEGMENTS, width), F32),
            pltpu.VMEM((vectors, 2, steps, width), F32),
            pltpu.VMEM((steps, vectors * fields * width), BF16),
            pltpu.VMEM((owners, 4, vectors, lanes), F32),
            pltpu.VMEM((parts, 4, vectors, lanes), F32),
            pltpu.VMEM((parts, 4, vectors, lanes), F32),
            pltpu.VMEM((owners, 4, vectors, lanes), F32),
            dma((8 + vectors * fields + 4 * BLOCKS,)),
            dma((8,)), dma((8,)),
            dma((4, 2)), dma((4, 2)),
            dma((12, chips // 2)), dma((12, chips // 2)),
            dma((2, chips)), dma((2, chips)),
            dma((BLOCKS, 2)), dma((BLOCKS, 2)),
            dma((owners,)), dma((parts,)), dma((parts,)), dma((owners,)),
        ],
        compiler_params=pltpu.CompilerParams(
            collective_id=0, has_side_effects=True, vmem_limit_bytes=VMEM_BYTES
        ),
        name="forward",
    )(eigenbasis, node_order.reshape(1, states), mu, eigenvalues.reshape(owners, 1, lanes), residual)

    tiles = 4
    tile = states // tiles
    return pl.pallas_call(
        backward_kernel,
        grid=(tiles,),
        in_specs=[
            pl.BlockSpec((2, BLOCKS, vectors * fields * steps, width), lambda i: (0, 0, 0, 0)),
            pl.BlockSpec((2, BLOCKS, tile, width), lambda i: (0, 0, i, 0)),
        ],
        out_specs=pl.BlockSpec((vectors, fields, steps, tile), lambda i: (0, 0, 0, i)),
        out_shape=jax.ShapeDtypeStruct((vectors, fields, steps, states), F32),
        compiler_params=pltpu.CompilerParams(vmem_limit_bytes=VMEM_BYTES),
        name="backward",
    )(back, moved)


def solution(mesh):
    placed = (P("grp", None, "tm", None), P("tm", None), P(), P())
    return jax.shard_map(
        on_device, mesh=mesh, in_specs=placed, out_specs=P("grp", None, "tm", None), check_vma=False
    )
```
